32 devices in a mesh: blk: 8 (over y, x, core), head: 4 (over z).
Axes of the slice: x: 2, y: 2, z: 4, core: 2. Of those that a mesh axis runs over, the one named last changes fastest.
Arguments:
- layer_input: bfloat16 [2, 8, 2, 256, 2048], P(None, 'blk', None, 'head'), may hold values from -6 to 6
- block_order: int32 [8], replicated, may hold values from 0 to 7, each once
- first_gain: bfloat16 [2048], P(('blk', 'head')), may hold values from 0.5 to 1.5
- first_shift: bfloat16 [2048], P(('blk', 'head')), may hold values from -1.5 to 1.5
- query_weight: bfloat16 [2048, 2048], P('blk', 'head'), may hold values from -0.125 to 0.125
- key_weight: bfloat16 [2048, 2048], P('blk', 'head'), may hold values from -0.125 to 0.125
- value_weight: bfloat16 [2048, 2048], P('blk', 'head'), may hold values from -0.125 to 0.125
- query_bias: bfloat16 [32, 64], P('head', 'blk'), may hold values from -2.5 to 2.5
- key_bias: bfloat16 [32, 16], P('head', 'blk'), may hold values from -2.5 to 2.5
- value_bias: bfloat16 [32, 64], P('head', 'blk'), may hold values from -2.5 to 2.5
- out_weight: bfloat16 [2048, 2048], P('head', 'blk'), may hold values from -1 to 1
- second_gain: bfloat16 [2048], P(('blk', 'head')), may hold values from 0.5 to 1.5
- second_shift: bfloat16 [2048], P(('blk', 'head')), may hold values from -1.5 to 1.5
- gate_weight: bfloat16 [2048, 5632], P('blk', 'head'), may hold values from -0.125 to 0.125
- up_weight: bfloat16 [2048, 5632], P('blk', 'head'), may hold values from -0.125 to 0.125
- down_weight: bfloat16 [5632, 2048], P('head', 'blk'), may hold values from -0.3125 to 0.3125
- out_grad: bfloat16 [2, 8, 2, 256, 2048], P(None, 'blk', None, 'head'), may hold values from -6 to 6
Outputs:
- layer_output: float32 [2, 8, 2, 256, 2048], P(None, 'blk', None, 'head')
- input_grad: float32 [2, 8, 2, 256, 2048], P(None, 'blk', None, 'head')
- first_gain_grad: float32 [2048], P(('blk', 'head'))
- first_shift_grad: float32 [2048], P(('blk', 'head'))
- query_weight_grad: float32 [2048, 2048], P('blk', 'head')
- key_weight_grad: float32 [2048, 2048], P('blk', 'head')
- value_weight_grad: float32 [2048, 2048], P('blk', 'head')
- query_bias_grad: float32 [32, 64], P('head', 'blk')
- key_bias_grad: float32 [32, 16], P('head', 'blk')
- value_bias_grad: float32 [32, 64], P('head', 'blk')
- out_weight_grad: float32 [2048, 2048], P('head', 'blk')
- second_gain_grad: float32 [2048], P(('blk', 'head'))
- second_shift_grad: float32 [2048], P(('blk', 'head'))
- gate_weight_grad: float32 [2048, 5632], P('blk', 'head')
- up_weight_grad: float32 [2048, 5632], P('blk', 'head')
- down_weight_grad: float32 [5632, 2048], P('head', 'blk')
The draws below stay inside these ranges and needn't reach their ends.
Inputs may be any that keep to these rules, and one draw needn't show every extreme that they name: A permutation: device b of blk holds blocks block_order[b] and 15 - block_order[b] of every sequence.
All inputs are finite; a program needn't handle non-finite values.
Results may differ from the reference program's by a relative error of at most 0.033.
Values may be sent and summed in bfloat16 or wider, within the bound.
No kernel may reach another device: no remote copies, remote signals or barrier semaphores. Data moves between devices by JAX's collectives and lax.ppermute only.
A program may use at most 192 MiB of HBM per device.

```python
import math
import jax
import jax.numpy as jnp
from jax import lax

D = 2048
HEADS = 32
HD = 64
ROT = 16
FF = 5632
SEQS = 2
CH = 256
LEN = 4096
N_BLK = 8


def level_of(stream_key, shape, pieces, least, largest):
    def one(axis_at, blocks):
        steps = jax.random.uniform(jax.random.fold_in(jax.random.fold_in(stream_key, 6), axis_at), (blocks,), jnp.float32, least / len(pieces), largest / len(pieces))
        return jnp.repeat(jnp.exp(steps), shape[axis_at] // blocks).reshape((-1,) + (1,) * (len(shape) - axis_at - 1))

    level = one(*pieces[0])
    for cut in pieces[1:]:
        level = level * one(*cut)
    return level


def centred(own_key, shape, width, most, cuts=(), kind=jnp.bfloat16):
    array = jax.random.normal(own_key, shape, jnp.float32) * width
    if len(cuts) > 0:
        array = level_of(own_key, shape, cuts, -0.22, 0.18) * array
    return jnp.clip(array, min=-most, max=most).astype(kind)


def setup_inputs(seed: int = 0) -> dict:
    streams_of = jax.random.split(jax.random.key(seed), 18)
    layer_input = centred(streams_of[0], (SEQS, N_BLK, 2, CH, D), 1.0, 6.0, ((1, 8), (3, 4)))
    block_order = jax.random.permutation(streams_of[1], N_BLK).astype(jnp.int32)
    first_gain = jnp.clip(1.0 + 0.1 * jax.random.normal(streams_of[2], (D,), jnp.float32), 0.5, 1.5).astype(jnp.bfloat16)
    first_shift = centred(streams_of[3], (D,), 0.3, 1.5, ((0, 32),))
    query_weight = centred(streams_of[4], (D, D), D ** -0.5, 0.125, ((0, 8), (1, 4)))
    key_weight = centred(streams_of[5], (D, D), D ** -0.5, 0.125, ((0, 8), (1, 4)))
    value_weight = centred(streams_of[6], (D, D), D ** -0.5, 0.125, ((0, 8), (1, 4)))
    query_bias = centred(streams_of[7], (HEADS, HD), 0.5, 2.5, ((0, 4), (1, 8)))
    key_bias = centred(streams_of[8], (HEADS, ROT), 0.5, 2.5, ((0, 4), (1, 8)))
    value_bias = centred(streams_of[9], (HEADS, HD), 0.5, 2.5, ((0, 4), (1, 8)))
    out_weight = centred(streams_of[10], (D, D), (D // 64) ** -0.5, 1.0, ((0, 4), (1, 8)))
    second_gain = jnp.clip(1.0 + 0.1 * jax.random.normal(streams_of[11], (D,), jnp.float32), 0.5, 1.5).astype(jnp.bfloat16)
    second_shift = centred(streams_of[12], (D,), 0.3, 1.5, ((0, 32),))
    gate_weight = centred(streams_of[13], (D, FF), D ** -0.5, 0.125, ((0, 8), (1, 4)))
    up_weight = centred(streams_of[14], (D, FF), D ** -0.5, 0.125, ((0, 8), (1, 4)))
    down_weight = centred(streams_of[15], (FF, D), (FF // 16) ** -0.5, 0.3125, ((0, 4), (1, 8)))
    out_grad = centred(streams_of[16], (SEQS, N_BLK, 2, CH, D), 1.0, 6.0, ((1, 8), (3, 4)))
    return {"layer_input": layer_input, "block_order": block_order, "first_gain": first_gain, "first_shift": first_shift, "query_weight": query_weight, "key_weight": key_weight, "value_weight": value_weight, "query_bias": query_bias, "key_bias": key_bias, "value_bias": value_bias, "out_weight": out_weight, "second_gain": second_gain, "second_shift": second_shift, "gate_weight": gate_weight, "up_weight": up_weight, "down_weight": down_weight, "out_grad": out_grad}


@jax.custom_vjp
def low(v):
    return lax.optimization_barrier(v.astype(jnp.bfloat16)).astype(jnp.float32)

@jax.custom_vjp
def low_back(v):
    return v

def low_keep(v):
    return (low(v), None)

def low_pass(kept, grad):
    return (grad,)

def back_keep(v):
    return (v, None)

def back_low(kept, grad):
    return (low(grad),)
low.defvjp(low_keep, low_pass)
low_back.defvjp(back_keep, back_low)
epsilon = 1e-05
masked_value = -1e+30
rotary_base = 10000.0

def matmul(left, right):
    return jnp.dot(left, right, precision=lax.Precision.HIGHEST)

def normalize(value, gain, shift):
    center = value - lax.optimization_barrier(jnp.mean(value, axis=-1, keepdims=True))
    inverse = lax.rsqrt(lax.optimization_barrier(jnp.mean(center * center, axis=-1, keepdims=True)) + epsilon)
    return center * inverse * gain + shift

def rotary_tables(positions):
    frequency = jnp.exp(jnp.arange(ROT // 2, dtype=jnp.float32) * (-2.0 * math.log(rotary_base) / ROT))
    phase_angle = positions.astype(jnp.float32)[:, None] * frequency[None, :]
    return (jnp.cos(phase_angle), jnp.sin(phase_angle))

def rotate(value, cosine, sine):
    half = ROT // 2
    first = value[..., :half]
    second = value[..., half:ROT]
    cosine = cosine[:, None, :]
    sine = sine[:, None, :]
    return jnp.concatenate([first * cosine - second * sine, second * cosine + first * sine, value[..., ROT:]], axis=-1)

def reference(layer_input, block_order, first_gain, first_shift, query_weight, key_weight, value_weight, query_bias, key_bias, value_bias, out_weight, second_gain, second_shift, gate_weight, up_weight, down_weight, out_grad):
    block_ids = jnp.stack([block_order, 2 * N_BLK - 1 - block_order], axis=1).reshape(-1).astype(jnp.int32)
    row_index = jnp.arange(LEN, dtype=jnp.int32)
    row_pos = block_ids[row_index // CH] * CH + row_index % CH
    holder = jnp.zeros((2 * N_BLK,), jnp.int32).at[block_ids].set(jnp.arange(2 * N_BLK, dtype=jnp.int32))
    pos_row = holder[row_index // CH] * CH + row_index % CH
    cosine, sine = rotary_tables(row_pos)
    query_block = math.gcd(LEN, 512)
    blocks_per_seq = LEN // query_block

    def forward(inputs, gain_one, shift_one, weight_query, weight_key, weight_value, bias_query, bias_key, bias_value, weight_out, gain_two, shift_two, weight_gate, weight_up, weight_down):
        normed_one = low(normalize(inputs, gain_one, shift_one)).reshape(-1, D)

        def heads_of(weight, bias):
            return (matmul(normed_one, weight) + bias.reshape(-1)).reshape(SEQS, LEN, HEADS, HD)
        full_key_bias = jnp.pad(bias_key, ((0, 0), (0, HD - ROT)))
        queries = low(rotate(low_back(heads_of(weight_query, bias_query)), cosine, sine))
        keys = low(rotate(low_back(heads_of(weight_key, full_key_bias)), cosine, sine))
        values = low(low_back(heads_of(weight_value, bias_value)))
        sorted_queries = queries[:, pos_row]
        sorted_keys = keys[:, pos_row]
        sorted_values = values[:, pos_row]

        def attend(block_index):
            seq_index = block_index // blocks_per_seq
            start = block_index % blocks_per_seq * query_block
            seq_queries = lax.dynamic_index_in_dim(sorted_queries, seq_index, 0, keepdims=False)
            seq_keys = lax.dynamic_index_in_dim(sorted_keys, seq_index, 0, keepdims=False)
            seq_values = lax.dynamic_index_in_dim(sorted_values, seq_index, 0, keepdims=False)
            block_queries = lax.dynamic_slice_in_dim(seq_queries, start, query_block, 0)
            scores = jnp.einsum('qhd,khd->hqk', block_queries, seq_keys, precision=lax.Precision.HIGHEST) / math.sqrt(HD)
            scores = low_back(scores)
            query_pos = start + jnp.arange(query_block, dtype=jnp.int32)
            key_pos = jnp.arange(LEN, dtype=jnp.int32)
            allowed = key_pos[None, None, :] <= query_pos[None, :, None]
            scores = jnp.where(allowed, scores, masked_value)
            weights_low = low(jax.nn.softmax(scores, axis=-1))
            return jnp.einsum('hqk,khd->qhd', weights_low, seq_values, precision=lax.Precision.HIGHEST)
        attended = lax.map(jax.checkpoint(attend), jnp.arange(SEQS * blocks_per_seq, dtype=jnp.int32))
        attended = attended.reshape(SEQS, LEN, HEADS, HD)[:, row_pos]
        attended_low = low(low_back(attended)).reshape(-1, D)
        middle = inputs + low_back(matmul(attended_low, weight_out)).reshape(inputs.shape)
        normed_two = low(normalize(middle, gain_two, shift_two)).reshape(-1, D)
        gate = low_back(matmul(normed_two, weight_gate))
        up_value = low_back(matmul(normed_two, weight_up))
        hidden = low(jax.nn.silu(gate) * up_value)
        return middle + low_back(matmul(hidden, weight_down)).reshape(inputs.shape)
    inputs = layer_input.astype(jnp.float32).reshape(SEQS, LEN, D)
    params = (first_gain, first_shift, query_weight, key_weight, value_weight, query_bias, key_bias, value_bias, out_weight, second_gain, second_shift, gate_weight, up_weight, down_weight)
    params = tuple((member.astype(jnp.float32) for member in params))
    result, pullback = jax.vjp(forward, inputs, *params)
    grads = pullback(out_grad.astype(jnp.float32).reshape(SEQS, LEN, D))
    return (result.reshape(layer_input.shape), grads[0].reshape(layer_input.shape), grads[1], grads[2], grads[3], grads[4], grads[5], grads[6], grads[7], grads[8], grads[9], grads[10], grads[11], grads[12], grads[13], grads[14])
```

```python
import functools
import math

import jax
import jax.numpy as jnp
from jax import lax
from jax.experimental import pallas as pl
from jax.experimental.pallas import tpu as pltpu
from jax.sharding import Mesh
from jax.sharding import PartitionSpec as P

HD = 64
ROT = 16

epsilon = 1e-05
masked_value = -1e30
rotary_base = 10000.0
log2_e = math.log2(math.e)
f32 = jnp.float32
bf16 = jnp.bfloat16
BLK = ("plane", "core")
ALL = ("plane", "core", "head")
MIB = 2**20


def dot(left, right, left_axis, right_axis):
    return lax.dot_general(
        left, right, (((left_axis,), (right_axis,)), ((), ())), preferred_element_type=f32
    )


def paired(value, axis, step):
    count = lax.axis_size(axis)
    return lax.ppermute(value, axis, [(source, source ^ step) for source in range(count)])


def exchange(value):
    planes = lax.axis_size("plane")
    value = value.reshape((planes, 2) + value.shape[1:])
    crossed = paired(value[:, 1], "core", 1)
    received = [jnp.stack([value[0, 0], crossed[0]])]
    for step in range(1, planes):
        received.append(paired(jnp.stack([value[step, 0], crossed[step]]), "plane", step))
    received = jnp.stack(received)
    return received.reshape((2 * planes,) + received.shape[2:])


def in_chain():
    return lax.axis_size("head") == 4


def head_offsets(part_rows):
    count = lax.axis_size("head")
    first = lax.axis_index("head") if in_chain() else 0
    part = (first + jnp.arange(count, dtype=jnp.int32)) % count
    inner = jnp.arange(part_rows, dtype=jnp.int32)
    return (part[:, None] * part_rows + inner[None, :]).reshape(-1)


def head_gather(value):
    if not in_chain():
        return lax.all_gather(value, "head", axis=1, tiled=True)
    index = lax.axis_index("head")
    two = lax.ppermute(value, "head", [(0, 2), (1, 3), (2, 0), (3, 1)])
    before = lax.ppermute(value, "head", [(0, 1), (1, 2), (2, 3)])
    after = lax.ppermute(value, "head", [(1, 0), (2, 1), (3, 2)])
    far = lax.ppermute(two, "head", [(1, 0), (2, 3)])
    return jnp.concatenate(
        [value, jnp.where(index == 3, far, after), two, jnp.where(index == 0, far, before)], axis=1
    )


def head_scatter(value):
    if not in_chain():
        return lax.psum_scatter(value, "head", scatter_dimension=1, tiled=True).astype(f32)
    index = lax.axis_index("head")
    own, after, two, before = jnp.split(value, 4, axis=1)
    far = lax.ppermute(
        jnp.where(index == 0, before, after), "head", [(0, 1), (3, 2)]
    )
    passed = (two.astype(f32) + far.astype(f32)).astype(bf16)
    from_two = lax.ppermute(passed, "head", [(0, 2), (1, 3), (2, 0), (3, 1)])
    from_before = lax.ppermute(after, "head", [(0, 1), (1, 2), (2, 3)])
    from_after = lax.ppermute(before, "head", [(1, 0), (2, 1), (3, 2)])
    return (own.astype(f32) + from_two.astype(f32)) + (
        from_before.astype(f32) + from_after.astype(f32)
    )


def blk_gather(value, axis=0):
    return lax.all_gather(value, BLK, axis=axis, tiled=True)


def blk_scatter(value, axis=0):
    return lax.psum_scatter(value.astype(bf16), BLK, scatter_dimension=axis, tiled=True).astype(f32)


def normalize(value, gain, shift):
    center = value - jnp.mean(value, axis=-1, keepdims=True)
    inverse = lax.rsqrt(jnp.mean(center * center, axis=-1, keepdims=True) + epsilon)
    return center * inverse * gain + shift


def norm_back(value, gain, upstream):
    center = value - jnp.mean(value, axis=-1, keepdims=True)
    inverse = lax.rsqrt(jnp.mean(center * center, axis=-1, keepdims=True) + epsilon)
    normed = center * inverse
    scaled = upstream * gain
    back = inverse * (
        scaled
        - jnp.mean(scaled, axis=-1, keepdims=True)
        - normed * jnp.mean(scaled * normed, axis=-1, keepdims=True)
    )
    return (back, jnp.sum(upstream * normed, axis=(0, 1)), jnp.sum(upstream, axis=(0, 1)))


def rotary_tables(positions):
    frequency = jnp.exp(
        jnp.arange(ROT // 2, dtype=jnp.float32) * (-2.0 * math.log(rotary_base) / ROT)
    )
    phase_angle = positions.astype(f32)[:, None, :] * frequency[None, :, None]
    return (jnp.cos(phase_angle), jnp.sin(phase_angle))


smem = pl.BlockSpec(memory_space=pltpu.SMEM)


def whole(shape):
    return pl.BlockSpec(shape, lambda step: (0,) * len(shape))


def compiler_params(mebibytes):
    return pltpu.CompilerParams(vmem_limit_bytes=mebibytes * MIB)


def project_in_kernel(
    blk_ref, rows_ref, query_ref, key_ref, value_ref, bias_q, bias_k, bias_v, cos_ref, sin_ref, out_ref
):
    group = pl.program_id(0)
    blk = blk_ref[0]
    halves = rows_ref.shape[0]
    heads = query_ref.shape[1] // HD
    copies = out_ref.shape[0] // (heads * pl.num_programs(0))
    half = ROT // 2
    for part, (weight, bias) in enumerate(
        ((query_ref, bias_q), (key_ref, bias_k), (value_ref, bias_v))
    ):
        for c in range(halves):
            result = dot(rows_ref[c], weight[...], 1, 0) + bias[...]
            result = result.T
            cosine, sine = cos_ref[c], sin_ref[c]
            for h in range(heads):
                values = result[h * HD : (h + 1) * HD]
                if part < 2:
                    first, second = values[:half], values[half:ROT]
                    values = jnp.concatenate(
                        [
                            first * cosine - second * sine,
                            second * cosine + first * sine,
                            values[ROT:],
                        ],
                        axis=0,
                    )
                values = values.astype(bf16)
                for copy in range(copies):
                    at = ((group * heads + h) * copies + copy) ^ blk
                    out_ref[at, c, part * HD : (part + 1) * HD, :] = values


def project_in(blk, rows, weight, bias, cosine, sine, devices):
    halves, ch, width = rows.shape
    total = weight.shape[1] // 3
    block = min(4 * HD, total)
    groups = total // block
    weights = [
        pl.BlockSpec((width, block), functools.partial(lambda p, g: (0, p * groups + g), part))
        for part in range(3)
    ]
    biases = [
        pl.BlockSpec((1, block), functools.partial(lambda p, g: (0, p * groups + g), part))
        for part in range(3)
    ]
    out = (devices, halves, 3 * HD, ch)
    return pl.pallas_call(
        project_in_kernel,
        grid=(groups,),
        in_specs=[smem, whole(rows.shape)]
        + weights
        + biases
        + [whole(cosine.shape), whole(sine.shape)],
        out_specs=whole(out),
        out_shape=jax.ShapeDtypeStruct(out, bf16),
        compiler_params=compiler_params(40),
        cost_estimate=pl.CostEstimate(
            flops=2 * halves * ch * width * 3 * total,
            bytes_accessed=2 * (rows.size + weight.size + math.prod(out)),
            transcendentals=0,
        ),
    )(blk, rows, weight, weight, weight, bias, bias, bias, cosine, sine)


def head_rows(ref, c, head, copies, blk):
    values = ref[(head * copies) ^ blk, c]
    if copies == 1:
        return values
    values = values.astype(f32)
    for copy in range(1, copies):
        values = values + ref[(head * copies + copy) ^ blk, c].astype(f32)
    return values.astype(bf16)


def project_out_kernel(blk_ref, attended_ref, weight_ref, out_ref, rows_ref, *, heads):
    blk = blk_ref[0]
    halves = out_ref.shape[0]
    copies = attended_ref.shape[0] // heads

    @pl.when(pl.program_id(0) == 0)
    def _():
        for c in range(halves):
            columns = [head_rows(attended_ref, c, h, copies, blk) for h in range(heads)]
            rows_ref[c] = jnp.concatenate(columns, axis=0).T

    for c in range(halves):
        out_ref[c] = dot(rows_ref[c], weight_ref[...], 1, 0).astype(bf16)


def project_out(blk, attended, weight):
    devices, halves, _, ch = attended.shape
    total, width = weight.shape
    block = min(1024, width)
    return pl.pallas_call(
        functools.partial(project_out_kernel, heads=total // HD),
        grid=(width // block,),
        in_specs=[
            smem,
            whole(attended.shape),
            pl.BlockSpec((total, block), lambda step: (0, step)),
        ],
        out_specs=[
            pl.BlockSpec((halves, ch, block), lambda step: (0, 0, step)),
            whole((halves, ch, total)),
        ],
        out_shape=[
            jax.ShapeDtypeStruct((halves, ch, width), bf16),
            jax.ShapeDtypeStruct((halves, ch, total), bf16),
        ],
        compiler_params=compiler_params(32),
        cost_estimate=pl.CostEstimate(
            flops=2 * halves * ch * width * total,
            bytes_accessed=2 * (attended.size + weight.size + halves * ch * (width + total)),
            transcendentals=0,
        ),
    )(blk, attended, weight)


def project_grad_kernel(blk_ref, rows_ref, weight_ref, out_ref):
    group = pl.program_id(0)
    blk = blk_ref[0]
    halves = rows_ref.shape[0]
    heads = weight_ref.shape[0] // HD
    copies = out_ref.shape[0] // (heads * pl.num_programs(0))
    for c in range(halves):
        result = dot(weight_ref[...], rows_ref[c], 1, 1).astype(bf16)
        for h in range(heads):
            for copy in range(copies):
                at = ((group * heads + h) * copies + copy) ^ blk
                out_ref[at, c] = result[h * HD : (h + 1) * HD]


def project_grad(blk, rows, weight, devices):
    halves, ch, width = rows.shape
    total = weight.shape[0]
    block = min(4 * HD, total)
    out = (devices, halves, HD, ch)
    return pl.pallas_call(
        project_grad_kernel,
        grid=(total // block,),
        in_specs=[
            smem,
            whole(rows.shape),
            pl.BlockSpec((block, width), lambda step: (step, 0)),
        ],
        out_specs=whole(out),
        out_shape=jax.ShapeDtypeStruct(out, bf16),
        compiler_params=compiler_params(32),
        cost_estimate=pl.CostEstimate(
            flops=2 * halves * ch * width * total,
            bytes_accessed=2 * (rows.size + weight.size + math.prod(out)),
            transcendentals=0,
        ),
    )(blk, rows, weight)


def project_back_kernel(blk_ref, grads_ref, weight_ref, out_ref, rows_ref, *, heads):
    blk = blk_ref[0]
    halves = out_ref.shape[0]
    copies = grads_ref.shape[0] // heads

    @pl.when(pl.program_id(0) == 0)
    def _():
        for c in range(halves):
            columns = [head_rows(grads_ref, c, h, copies, blk) for h in range(heads)]
            for part in range(3):
                rows_ref[c, :, part * heads * HD : (part + 1) * heads * HD] = jnp.concatenate(
                    [column[part * HD : (part + 1) * HD] for column in columns], axis=0
                ).T

    for c in range(halves):
        out_ref[c] = dot(rows_ref[c], weight_ref[...], 1, 1).astype(bf16)


def project_back(blk, grads, weight):
    devices, halves, _, ch = grads.shape
    width, total = weight.shape
    block = min(512, width)
    return pl.pallas_call(
        functools.partial(project_back_kernel, heads=total // (3 * HD)),
        grid=(width // block,),
        in_specs=[
            smem,
            whole(grads.shape),
            pl.BlockSpec((block, total), lambda step: (step, 0)),
        ],
        out_specs=[
            pl.BlockSpec((halves, ch, block), lambda step: (0, 0, step)),
            whole((halves, ch, total)),
        ],
        out_shape=[
            jax.ShapeDtypeStruct((halves, ch, width), bf16),
            jax.ShapeDtypeStruct((halves, ch, total), bf16),
        ],
        compiler_params=compiler_params(32),
        cost_estimate=pl.CostEstimate(
            flops=2 * halves * ch * width * total,
            bytes_accessed=2 * (grads.size + weight.size + halves * ch * (width + total)),
            transcendentals=0,
        ),
    )(blk, grads, weight)


def attend_kernel(
    place_ref, tiles_ref, along_ref, down_ref, qkv_ref, out_ref, exact_ref, lse_ref, keys, queries, values
):
    blocks, _, ch = qkv_ref.shape
    span = 2 * ch
    tiles = blocks // 2
    mine = tiles_ref.shape[0]
    if mine < tiles:
        out_ref[...] = jnp.zeros(out_ref.shape, out_ref.dtype)
        exact_ref[...] = jnp.zeros(exact_ref.shape, exact_ref.dtype)
        lse_ref[...] = jnp.zeros(lse_ref.shape, lse_ref.dtype)

    def arrange(t, unused):
        for half in range(2):
            block = qkv_ref[place_ref[2 * t + half]]
            columns = slice(half * ch, (half + 1) * ch)
            queries[t, :, columns] = block[:HD]
            keys[t, columns, :] = block[HD : 2 * HD].T
            values[t, :, columns] = block[2 * HD :]
        return unused

    lax.fori_loop(0, tiles, arrange, 0)
    scale = log2_e * HD**-0.5

    def query_tile(step, unused):
        t = tiles_ref[step]
        query = queries[t]

        def visit(j, carry, diagonal=False):
            peak, total, acc = carry
            scores = dot(keys[j], query, 1, 0) * scale
            if diagonal:
                scores = jnp.where(down_ref[...] <= along_ref[...], scores, masked_value)
            new_peak = jnp.maximum(peak, jnp.max(scores, axis=0, keepdims=True))
            weights = jnp.exp2(scores - new_peak)
            shrink = jnp.exp2(peak - new_peak)
            total = total * shrink + jnp.sum(weights, axis=0, keepdims=True)
            acc = acc * shrink + dot(values[j], weights.astype(bf16), 1, 0)
            return new_peak, total, acc

        carry = (
            jnp.full((1, span), masked_value, f32),
            jnp.zeros((1, span), f32),
            jnp.zeros((HD, span), f32),
        )
        carry = visit(t, carry, True)
        peak, total, acc = lax.fori_loop(0, t, visit, carry)
        result = acc / total
        lse = peak + jnp.log2(total)
        for half in range(2):
            at = place_ref[2 * t + half]
            columns = slice(half * ch, (half + 1) * ch)
            exact_ref[at] = result[:, columns]
            out_ref[at] = result[:, columns].astype(bf16)
            lse_ref[at] = lse[:, columns]
        return unused

    lax.fori_loop(0, mine, query_tile, 0)


vmem = pl.BlockSpec(memory_space=pltpu.VMEM)


def attend(place, tiles, along, down, qkv):
    blocks, _, ch = qkv.shape
    n = blocks // 2
    return pl.pallas_call(
        attend_kernel,
        in_specs=[smem, smem] + [vmem] * 3,
        out_specs=[vmem] * 3,
        out_shape=[
            jax.ShapeDtypeStruct((blocks, HD, ch), bf16),
            jax.ShapeDtypeStruct((blocks, HD, ch), f32),
            jax.ShapeDtypeStruct((blocks, 1, ch), f32),
        ],
        scratch_shapes=[
            pltpu.VMEM((n, 2 * ch, HD), bf16),
            pltpu.VMEM((n, HD, 2 * ch), bf16),
            pltpu.VMEM((n, HD, 2 * ch), bf16),
        ],
        compiler_params=compiler_params(40),
        cost_estimate=pl.CostEstimate(
            flops=blocks * blocks * ch * ch * HD * 8,
            bytes_accessed=blocks * ch * HD * 12,
            transcendentals=blocks * blocks * ch * ch // 2,
        ),
    )(place, tiles, along, down, qkv)


def unrotate(values, cosine, sine):
    half = ROT // 2
    first, second = values[:half], values[half:ROT]
    return jnp.concatenate(
        [first * cosine + second * sine, second * cosine - first * sine, values[ROT:]], axis=0
    )


def attend_back_kernel(
    place_ref,
    tiles_ref,
    along_ref,
    down_ref,
    qkv_ref,
    grad_ref,
    exact_ref,
    lse_ref,
    cos_ref,
    sin_ref,
    out_ref,
    sums_ref,
    keys_t,
    keys,
    queries_t,
    queries,
    values,
    grads_t,
    grads,
    lse,
    delta,
    grad_q,
    grad_k,
    grad_v,
):
    blocks, _, ch = qkv_ref.shape
    span = 2 * ch
    tiles = blocks // 2
    mine = tiles_ref.shape[0]

    def arrange(t, unused):
        for half in range(2):
            at = place_ref[2 * t + half]
            block = qkv_ref[at]
            columns = slice(half * ch, (half + 1) * ch)
            queries_t[t, :, columns] = block[:HD]
            queries[t, columns, :] = block[:HD].T
            keys_t[t, :, columns] = block[HD : 2 * HD]
            keys[t, columns, :] = block[HD : 2 * HD].T
            values[t, columns, :] = block[2 * HD :].T
            grad = grad_ref[at]
            grads_t[t, :, columns] = grad
            grads[t, columns, :] = grad.T
            lse[t, :, columns] = lse_ref[at]
            delta[t, :, columns] = jnp.sum(grad.astype(f32) * exact_ref[at], axis=0, keepdims=True)
        grad_q[t] = jnp.zeros(grad_q.shape[1:], f32)
        grad_k[t] = jnp.zeros(grad_k.shape[1:], f32)
        grad_v[t] = jnp.zeros(grad_v.shape[1:], f32)
        return unused

    lax.fori_loop(0, tiles, arrange, 0)
    factor = HD**-0.5
    scale = log2_e * factor

    def query_tile(step, unused):
        t = tiles_ref[step]

        def visit(j, acc, diagonal=False):
            scores = dot(keys[j], queries_t[t], 1, 0) * scale
            weights = jnp.exp2(scores - lse[t])
            if diagonal:
                weights = jnp.where(down_ref[...] <= along_ref[...], weights, 0.0)
            grad_weights = dot(values[j], grads_t[t], 1, 0)
            grad_scores = (weights * (grad_weights - delta[t])).astype(bf16)
            grad_v[j] += dot(weights.astype(bf16), grads[t], 1, 0)
            grad_k[j] += dot(grad_scores, queries[t], 1, 0)
            return acc + dot(keys_t[j], grad_scores, 1, 0)

        acc = visit(t, jnp.zeros((HD, span), f32), True)
        grad_q[t] = lax.fori_loop(0, t, visit, acc)
        return unused

    lax.fori_loop(0, mine, query_tile, 0)

    def finish(t, sums):
        key_t = grad_k[t].T
        value_t = grad_v[t].T
        for half in range(2):
            at = place_ref[2 * t + half]
            columns = slice(half * ch, (half + 1) * ch)
            cosine, sine = cos_ref[2 * t + half], sin_ref[2 * t + half]
            parts = (
                unrotate(grad_q[t][:, columns] * factor, cosine, sine),
                unrotate(key_t[:, columns] * factor, cosine, sine),
                value_t[:, columns],
            )
            rows = jnp.concatenate(parts, axis=0).astype(bf16)
            out_ref[at] = rows
            sums = sums + rows.astype(f32)
        return sums

    sums = lax.fori_loop(0, tiles, finish, jnp.zeros((3 * HD, ch), f32))
    sums_ref[...] = jnp.sum(sums, axis=1, keepdims=True)


def attend_back(place, tiles, along, down, qkv, grad, exact, lse, cosine, sine):
    blocks, _, ch = qkv.shape
    n = blocks // 2
    flat = pltpu.VMEM((n, HD, 2 * ch), bf16)
    tall = pltpu.VMEM((n, 2 * ch, HD), bf16)
    line = pltpu.VMEM((n, 1, 2 * ch), f32)
    return pl.pallas_call(
        attend_back_kernel,
        in_specs=[smem, smem] + [vmem] * 8,
        out_specs=[vmem] * 2,
        out_shape=[
            jax.ShapeDtypeStruct((blocks, 3 * HD, ch), bf16),
            jax.ShapeDtypeStruct((3 * HD, 1), f32),
        ],
        scratch_shapes=[
            flat,
            tall,
            flat,
            tall,
            tall,
            flat,
            tall,
            line,
            line,
            pltpu.VMEM((n, HD, 2 * ch), f32),
            pltpu.VMEM((n, 2 * ch, HD), f32),
            pltpu.VMEM((n, 2 * ch, HD), f32),
        ],
        compiler_params=compiler_params(48),
        cost_estimate=pl.CostEstimate(
            flops=blocks * blocks * ch * ch * HD * 20,
            bytes_accessed=blocks * ch * HD * 24,
            transcendentals=blocks * blocks * ch * ch // 2,
        ),
    )(place, tiles, along, down, qkv, grad, exact, lse, cosine, sine)


def local(
    layer_input,
    block_order,
    first_gain,
    first_shift,
    query_weight,
    key_weight,
    value_weight,
    query_bias,
    key_bias,
    value_bias,
    out_weight,
    second_gain,
    second_shift,
    gate_weight,
    up_weight,
    down_weight,
    out_grad,
):
    seqs, _, halves, part_rows, width = layer_input.shape
    planes = lax.axis_size("plane")
    devices = 2 * planes
    head_size = lax.axis_size("head")
    blk = lax.axis_index("plane") * 2 + lax.axis_index("core")
    head_index = lax.axis_index("head")
    blk_scalar = blk.astype(jnp.int32).reshape(1)
    ch = part_rows * head_size
    blocks = halves * devices
    heads = query_bias.shape[0]
    local_width = heads * HD
    copies = devices // heads

    part = first_gain.shape[0]
    small = jnp.concatenate(
        [first_gain, first_shift, second_gain, second_shift]
        + [member.reshape(-1) for member in (query_bias, key_bias, value_bias)]
    )
    small = lax.all_gather(small, ALL, axis=0, tiled=False).astype(f32)
    gain_one, shift_one, gain_two, shift_two = [
        small[:, k * part : (k + 1) * part].reshape(-1) for k in range(4)
    ]
    biases = lax.dynamic_index_in_dim(
        small[:, 4 * part :].reshape(devices, head_size, -1), head_index, 1, keepdims=False
    )

    def bias_of(start, dims):
        member = biases[:, start : start + heads * dims].reshape(devices, heads, dims)
        return jnp.swapaxes(member, 0, 1).reshape(heads, devices * dims)

    q_dims, k_dims = query_bias.shape[1], key_bias.shape[1]
    bias_query = bias_of(0, q_dims)
    bias_key = jnp.pad(bias_of(heads * q_dims, k_dims), ((0, 0), (0, HD - ROT)))
    bias_value = bias_of(heads * (q_dims + k_dims), q_dims)
    bias = jnp.concatenate([bias_query, bias_key, bias_value], axis=0).reshape(1, -1)

    owner = jnp.arange(devices, dtype=jnp.int32) ^ blk
    first_id = block_order[owner]
    rank = jnp.stack([first_id, 2 * devices - 1 - first_id], axis=1).reshape(-1)
    place = jnp.zeros((blocks,), jnp.int32).at[rank].set(jnp.arange(blocks, dtype=jnp.int32))
    offsets = head_offsets(part_rows)
    own_positions = rank[:halves, None] * ch + offsets[None, :]
    cos_own, sin_own = rotary_tables(own_positions)
    all_positions = jnp.arange(blocks, dtype=jnp.int32)[:, None] * ch + offsets[None, :]
    cos_all, sin_all = rotary_tables(all_positions)
    along = all_positions[:2].reshape(1, -1)
    down = all_positions[:2].reshape(-1, 1)
    tile_count = blocks // 2
    cycle = jnp.arange(tile_count // copies, dtype=jnp.int32)
    share = blk % copies
    tiles = (cycle // 2) * 2 * copies + jnp.where(cycle % 2 == 0, share, 2 * copies - 1 - share)
    if copies == 1:
        tiles = jnp.arange(tile_count, dtype=jnp.int32)

    full_qkv = blk_gather(jnp.concatenate([query_weight, key_weight, value_weight], axis=1))
    full_out = blk_gather(out_weight, 1)
    full_gate = blk_gather(gate_weight)
    full_up = blk_gather(up_weight)
    full_down = blk_gather(down_weight, 1)

    each = range(seqs)
    rows_in = [layer_input[s, 0].astype(f32) for s in each]
    grad_own = [out_grad[s, 0] for s in each]
    rows_one = [head_gather(normalize(rows_in[s], gain_one, shift_one).astype(bf16)) for s in each]
    qkv = [
        exchange(project_in(blk_scalar, rows_one[s], full_qkv, bias, cos_own, sin_own, devices))
        for s in each
    ]
    qkv = [member.reshape(blocks, 3 * HD, ch) for member in qkv]
    grad_rows = [head_gather(grad_own[s]) for s in each]
    attended = [attend(place, tiles, along, down, qkv[s]) for s in each]
    middle = []
    out_rows = []
    rows_two = []
    for s in each:
        moved = exchange(attended[s][0].reshape(devices, halves, HD, ch))
        summand, rows = project_out(blk_scalar, moved, full_out)
        out_rows.append(rows)
        middle.append(rows_in[s] + head_scatter(summand))
        rows_two.append(
            head_gather(normalize(middle[s], gain_two, shift_two).astype(bf16)).reshape(-1, width)
        )

    layer_output = []
    hiddens, grad_gates, grad_ups, grad_middle, norm_two_grads, grad_branch = [], [], [], [], [], []
    for s in each:
        flat_grad = grad_rows[s].reshape(-1, width)
        gate = dot(rows_two[s], full_gate, 1, 0)
        up_value = dot(rows_two[s], full_up, 1, 0)
        sigmoid_gate = jax.nn.sigmoid(gate)
        silu_gate = gate * sigmoid_gate
        hidden = (silu_gate * up_value).astype(bf16)
        summand = dot(hidden, full_down, 1, 0).astype(bf16)
        layer_output.append(middle[s] + head_scatter(summand.reshape(halves, ch, width)))
        grad_hidden = dot(flat_grad, full_down, 1, 1)
        grad_up = (grad_hidden * silu_gate).astype(bf16)
        grad_gate = (
            grad_hidden * up_value * sigmoid_gate * (1.0 + gate * (1.0 - sigmoid_gate))
        ).astype(bf16)
        summand = (dot(grad_gate, full_gate, 1, 1) + dot(grad_up, full_up, 1, 1)).astype(bf16)
        grad_normed_two = head_scatter(summand.reshape(halves, ch, width))
        back, gain_grad, shift_grad = norm_back(middle[s], gain_two, grad_normed_two)
        grad_middle.append(grad_own[s].astype(f32) + back)
        norm_two_grads.append((gain_grad, shift_grad))
        grad_branch.append(head_gather(grad_middle[s].astype(bf16)))
        hiddens.append(hidden)
        grad_gates.append(grad_gate)
        grad_ups.append(grad_up)

    def summed_dot(lefts, rights):
        total = dot(lefts[0], rights[0], 0, 0)
        for s in range(1, seqs):
            total = total + dot(lefts[s], rights[s], 0, 0)
        return total

    flat_grads = [member.reshape(-1, width) for member in grad_rows]
    down_grad = blk_scatter(summed_dot(hiddens, flat_grads), 1)
    gate_grad = blk_scatter(summed_dot(rows_two, grad_gates))
    up_grad = blk_scatter(summed_dot(rows_two, grad_ups))
    flat_branch = [member.reshape(-1, width) for member in grad_branch]
    flat_out_rows = [member.reshape(-1, local_width) for member in out_rows]
    out_weight_grad = blk_scatter(summed_dot(flat_out_rows, flat_branch), 1)

    input_grad, norm_one_grads, qkv_rows, bias_sums = [], [], [], []
    for s in each:
        grad_heads = exchange(project_grad(blk_scalar, grad_branch[s], full_out, devices))
        _, exact, lse = attended[s]
        qkv_grad, sums = attend_back(
            place,
            tiles,
            along,
            down,
            qkv[s],
            grad_heads.reshape(blocks, HD, ch),
            exact,
            lse,
            cos_all,
            sin_all,
        )
        bias_sums.append(sums)
        moved = exchange(qkv_grad.reshape(devices, halves, 3 * HD, ch))
        summand, rows = project_back(blk_scalar, moved, full_qkv)
        qkv_rows.append(rows.reshape(-1, 3 * local_width))
        back, gain_grad, shift_grad = norm_back(rows_in[s], gain_one, head_scatter(summand))
        norm_one_grads.append((gain_grad, shift_grad))
        input_grad.append(grad_middle[s] + back)
    qkv_grad = blk_scatter(
        summed_dot([member.reshape(-1, width) for member in rows_one], qkv_rows)
    )

    def over_all(grads, k):
        total = grads[0][k]
        for s in range(1, seqs):
            total = total + grads[s][k]
        return total.reshape(devices * head_size, part)

    bias_total = bias_sums[0]
    for s in range(1, seqs):
        bias_total = bias_total + bias_sums[s]
    bias_total = bias_total.reshape(3, HD)
    shares = jnp.concatenate(
        [
            bias_total[0].reshape(devices, q_dims),
            bias_total[1, :ROT].reshape(devices, k_dims),
            bias_total[2].reshape(devices, q_dims),
        ],
        axis=1,
    )
    own_head = (jnp.arange(heads, dtype=jnp.int32) == blk // copies).astype(f32)
    own_column = (jnp.arange(head_size, dtype=jnp.int32) == head_index).astype(f32)
    spread = (
        shares[:, None, None, :] * own_head[None, None, :, None] * own_column[None, :, None, None]
    ).reshape(devices * head_size, -1)
    smalls = jnp.concatenate(
        [
            over_all(norm_one_grads, 0),
            over_all(norm_one_grads, 1),
            over_all(norm_two_grads, 0),
            over_all(norm_two_grads, 1),
            spread,
        ],
        axis=1,
    )
    smalls = lax.psum_scatter(smalls, ALL, scatter_dimension=0, tiled=True).reshape(-1)
    norm_grads = [smalls[k * part : (k + 1) * part] for k in range(4)]
    bias_grads = smalls[4 * part :].reshape(heads, 2 * q_dims + k_dims)
    stacked = lambda members: jnp.stack(members)[:, None]
    return (
        stacked(layer_output),
        stacked(input_grad),
        norm_grads[0],
        norm_grads[1],
        qkv_grad[:, :local_width],
        qkv_grad[:, local_width : 2 * local_width],
        qkv_grad[:, 2 * local_width :],
        bias_grads[:, :q_dims],
        bias_grads[:, q_dims : q_dims + k_dims],
        bias_grads[:, q_dims + k_dims :],
        out_weight_grad,
        norm_grads[2],
        norm_grads[3],
        gate_grad,
        up_grad,
        down_grad,
    )


def solution(mesh):
    blk_size, head_size = mesh.devices.shape
    split = Mesh(mesh.devices.reshape(blk_size // 2, 2, head_size), ALL)
    tokens = P(None, BLK, None, "head", None)
    rows = P(BLK, "head")
    columns = P("head", BLK)
    return jax.shard_map(
        local,
        mesh=split,
        in_specs=(
            tokens,
            P(),
            P(ALL),
            P(ALL),
            rows,
            rows,
            rows,
            columns,
            columns,
            columns,
            columns,
            P(ALL),
            P(ALL),
            rows,
            rows,
            columns,
            tokens,
        ),
        out_specs=(
            tokens,
            tokens,
            P(ALL),
            P(ALL),
            rows,
            rows,
            rows,
            columns,
            columns,
            columns,
            columns,
            P(ALL),
            P(ALL),
            rows,
            rows,
            columns,
        ),
        check_vma=False,
    )
```

```python
import functools
import math

import jax
import jax.numpy as jnp
from jax import lax
from jax.experimental import pallas as pl
from jax.experimental.pallas import tpu as pltpu
from jax.sharding import Mesh
from jax.sharding import PartitionSpec as P

HD = 64
ROT = 16

epsilon = 1e-05
masked_value = -1e30
rotary_base = 10000.0
log2_e = math.log2(math.e)
f32 = jnp.float32
bf16 = jnp.bfloat16
BLK = ("plane", "core")
ALL = ("plane", "core", "head")
MIB = 2**20


def dot(left, right, left_axis, right_axis):
    return lax.dot_general(
        left, right, (((left_axis,), (right_axis,)), ((), ())), preferred_element_type=f32
    )


def paired(value, axis, step):
    count = lax.axis_size(axis)
    return lax.ppermute(value, axis, [(source, source ^ step) for source in range(count)])


def exchange(value):
    planes = lax.axis_size("plane")
    value = value.reshape((planes, 2) + value.shape[1:])
    crossed = paired(value[:, 1], "core", 1)
    received = [jnp.stack([value[0, 0], crossed[0]])]
    for step in range(1, planes):
        received.append(paired(jnp.stack([value[step, 0], crossed[step]]), "plane", step))
    received = jnp.stack(received)
    return received.reshape((2 * planes,) + received.shape[2:])


def steps_of(axes):
    for axis in reversed(axes):
        step = 1
        while step < lax.axis_size(axis):
            yield axis, step
            step *= 2


def small_gather(value, axes):
    for axis, step in steps_of(axes):
        other = paired(value, axis, step)
        low = (lax.axis_index(axis) & step) == 0
        value = jnp.concatenate([jnp.where(low, value, other), jnp.where(low, other, value)])
    return value


def small_scatter(value):
    shape = value.shape[1:]
    for axis, step in steps_of(ALL):
        value = value.reshape((-1, 2) + shape)
        low = (lax.axis_index(axis) & step) == 0
        keep = jnp.where(low, value[:, 0], value[:, 1])
        value = keep + paired(jnp.where(low, value[:, 1], value[:, 0]), axis, step)
    return value.reshape(shape)


def in_chain():
    return lax.axis_size("head") == 4


def head_order():
    first = lax.axis_index("head") if in_chain() else 0
    return first ^ jnp.arange(lax.axis_size("head"), dtype=jnp.int32)


def head_offsets(part_rows):
    inner = jnp.arange(part_rows, dtype=jnp.int32)
    return (head_order()[:, None] * part_rows + inner[None, :]).reshape(-1)


def in_head_order(value, axis):
    if not in_chain():
        return value
    order = head_order()
    rows = value.shape[axis] // lax.axis_size("head")
    return jnp.concatenate(
        [
            lax.dynamic_slice_in_dim(value, order[k] * rows, rows, axis)
            for k in range(lax.axis_size("head"))
        ],
        axis=axis,
    )


ONE = [(0, 1), (1, 0), (2, 3), (3, 2)]
TWO = [(0, 2), (1, 3), (2, 0), (3, 1)]
MIDDLE = [(1, 2), (2, 1)]
OUTWARD = [(1, 0), (2, 3)]
INWARD = [(0, 1), (3, 2)]


def gather_first(value):
    if not in_chain():
        return value
    return lax.ppermute(value, "head", TWO), lax.ppermute(value, "head", ONE)


def gather_rest(value, received):
    if not in_chain():
        return lax.all_gather(value, "head", axis=1, tiled=True)
    two, one = received
    return (
        value,
        one,
        two,
        lax.ppermute(two, "head", OUTWARD),
        lax.ppermute(value, "head", MIDDLE),
    )


def gather_whole(parts):
    if not in_chain():
        return parts
    value, one, two, far, near = parts
    index = lax.axis_index("head")
    last = jnp.where((index == 0) | (index == 3), far, near)
    return jnp.concatenate([value, one, two, last], axis=1)


def scatter_first(value):
    if not in_chain():
        return value
    own, one, two, last = jnp.split(value, 4, axis=1)
    return (
        own,
        one,
        two,
        lax.ppermute(last, "head", INWARD),
        lax.ppermute(last, "head", MIDDLE),
    )


def scatter_rest(parts):
    if not in_chain():
        return lax.psum_scatter(parts, "head", scatter_dimension=1, tiled=True)
    own, one, two, far, near = parts
    passed = (two.astype(f32) + far.astype(f32)).astype(bf16)
    return own, lax.ppermute(passed, "head", TWO), lax.ppermute(one, "head", ONE), near


def scatter_whole(parts):
    if not in_chain():
        return parts.astype(f32)
    own, two, one, near = [member.astype(f32) for member in parts]
    return (own + two) + (one + near)


def blk_gather(value, axis=0):
    return lax.all_gather(value, BLK, axis=axis, tiled=True)


def blk_scatter(value, axis=0):
    return lax.psum_scatter(value.astype(bf16), BLK, scatter_dimension=axis, tiled=True).astype(f32)


def normalize(value, gain, shift):
    center = value - jnp.mean(value, axis=-1, keepdims=True)
    inverse = lax.rsqrt(jnp.mean(center * center, axis=-1, keepdims=True) + epsilon)
    return center * inverse * gain + shift


def norm_back(value, gain, upstream):
    center = value - jnp.mean(value, axis=-1, keepdims=True)
    inverse = lax.rsqrt(jnp.mean(center * center, axis=-1, keepdims=True) + epsilon)
    normed = center * inverse
    scaled = upstream * gain
    back = inverse * (
        scaled
        - jnp.mean(scaled, axis=-1, keepdims=True)
        - normed * jnp.mean(scaled * normed, axis=-1, keepdims=True)
    )
    return (back, jnp.sum(upstream * normed, axis=(0, 1)), jnp.sum(upstream, axis=(0, 1)))


def rotary_tables(positions):
    frequency = jnp.exp(
        jnp.arange(ROT // 2, dtype=jnp.float32) * (-2.0 * math.log(rotary_base) / ROT)
    )
    phase_angle = positions.astype(f32)[:, None, :] * frequency[None, :, None]
    return (jnp.cos(phase_angle), jnp.sin(phase_angle))


smem = pl.BlockSpec(memory_space=pltpu.SMEM)


def whole(shape):
    return pl.BlockSpec(shape, lambda step: (0,) * len(shape))


def compiler_params(mebibytes):
    return pltpu.CompilerParams(vmem_limit_bytes=mebibytes * MIB)


def project_in_kernel(
    blk_ref, rows_ref, query_ref, key_ref, value_ref, bias_q, bias_k, bias_v, cos_ref, sin_ref, out_ref
):
    group = pl.program_id(0)
    blk = blk_ref[0]
    halves = rows_ref.shape[0]
    heads = query_ref.shape[1] // HD
    copies = out_ref.shape[0] // (heads * pl.num_programs(0))
    half = ROT // 2
    for part, (weight, bias) in enumerate(
        ((query_ref, bias_q), (key_ref, bias_k), (value_ref, bias_v))
    ):
        for c in range(halves):
            result = dot(rows_ref[c], weight[...], 1, 0) + bias[...]
            result = result.T
            cosine, sine = cos_ref[c], sin_ref[c]
            for h in range(heads):
                values = result[h * HD : (h + 1) * HD]
                if part < 2:
                    first, second = values[:half], values[half:ROT]
                    values = jnp.concatenate(
                        [
                            first * cosine - second * sine,
                            second * cosine + first * sine,
                            values[ROT:],
                        ],
                        axis=0,
                    )
                values = values.astype(bf16)
                for copy in range(copies):
                    at = ((group * heads + h) * copies + copy) ^ blk
                    out_ref[at, c, part * HD : (part + 1) * HD, :] = values


def project_in(blk, rows, weight, bias, cosine, sine, devices):
    halves, ch, width = rows.shape
    total = weight.shape[1] // 3
    block = min(4 * HD, total)
    groups = total // block
    weights = [
        pl.BlockSpec((width, block), functools.partial(lambda p, g: (0, p * groups + g), part))
        for part in range(3)
    ]
    biases = [
        pl.BlockSpec((1, block), functools.partial(lambda p, g: (0, p * groups + g), part))
        for part in range(3)
    ]
    out = (devices, halves, 3 * HD, ch)
    return pl.pallas_call(
        project_in_kernel,
        grid=(groups,),
        in_specs=[smem, whole(rows.shape)]
        + weights
        + biases
        + [whole(cosine.shape), whole(sine.shape)],
        out_specs=whole(out),
        out_shape=jax.ShapeDtypeStruct(out, bf16),
        compiler_params=compiler_params(40),
        cost_estimate=pl.CostEstimate(
            flops=2 * halves * ch * width * 3 * total,
            bytes_accessed=2 * (rows.size + weight.size + math.prod(out)),
            transcendentals=0,
        ),
    )(blk, rows, weight, weight, weight, bias, bias, bias, cosine, sine)


def head_rows(ref, c, head, copies, blk):
    values = ref[(head * copies) ^ blk, c]
    if copies == 1:
        return values
    values = values.astype(f32)
    for copy in range(1, copies):
        values = values + ref[(head * copies + copy) ^ blk, c].astype(f32)
    return values.astype(bf16)


def project_out_kernel(blk_ref, attended_ref, weight_ref, out_ref, rows_ref, *, heads):
    blk = blk_ref[0]
    halves = out_ref.shape[0]
    copies = attended_ref.shape[0] // heads

    @pl.when(pl.program_id(0) == 0)
    def _():
        for c in range(halves):
            columns = [head_rows(attended_ref, c, h, copies, blk) for h in range(heads)]
            rows_ref[c] = jnp.concatenate(columns, axis=0).T

    for c in range(halves):
        out_ref[c] = dot(rows_ref[c], weight_ref[...], 1, 0).astype(bf16)


def project_out(blk, attended, weight):
    devices, halves, _, ch = attended.shape
    total, width = weight.shape
    block = min(1024, width)
    return pl.pallas_call(
        functools.partial(project_out_kernel, heads=total // HD),
        grid=(width // block,),
        in_specs=[
            smem,
            whole(attended.shape),
            pl.BlockSpec((total, block), lambda step: (0, step)),
        ],
        out_specs=[
            pl.BlockSpec((halves, ch, block), lambda step: (0, 0, step)),
            whole((halves, ch, total)),
        ],
        out_shape=[
            jax.ShapeDtypeStruct((halves, ch, width), bf16),
            jax.ShapeDtypeStruct((halves, ch, total), bf16),
        ],
        compiler_params=compiler_params(32),
        cost_estimate=pl.CostEstimate(
            flops=2 * halves * ch * width * total,
            bytes_accessed=2 * (attended.size + weight.size + halves * ch * (width + total)),
            transcendentals=0,
        ),
    )(blk, attended, weight)


def project_grad_kernel(blk_ref, rows_ref, weight_ref, out_ref):
    group = pl.program_id(0)
    blk = blk_ref[0]
    halves = rows_ref.shape[0]
    heads = weight_ref.shape[0] // HD
    copies = out_ref.shape[0] // (heads * pl.num_programs(0))
    for c in range(halves):
        result = dot(weight_ref[...], rows_ref[c], 1, 1).astype(bf16)
        for h in range(heads):
            for copy in range(copies):
                at = ((group * heads + h) * copies + copy) ^ blk
                out_ref[at, c] = result[h * HD : (h + 1) * HD]


def project_grad(blk, rows, weight, devices):
    halves, ch, width = rows.shape
    total = weight.shape[0]
    block = min(4 * HD, total)
    out = (devices, halves, HD, ch)
    return pl.pallas_call(
        project_grad_kernel,
        grid=(total // block,),
        in_specs=[
            smem,
            whole(rows.shape),
            pl.BlockSpec((block, width), lambda step: (step, 0)),
        ],
        out_specs=whole(out),
        out_shape=jax.ShapeDtypeStruct(out, bf16),
        compiler_params=compiler_params(32),
        cost_estimate=pl.CostEstimate(
            flops=2 * halves * ch * width * total,
            bytes_accessed=2 * (rows.size + weight.size + math.prod(out)),
            transcendentals=0,
        ),
    )(blk, rows, weight)


def project_back_kernel(blk_ref, grads_ref, weight_ref, out_ref, rows_ref, *, heads):
    blk = blk_ref[0]
    halves = out_ref.shape[0]
    copies = grads_ref.shape[0] // heads

    @pl.when(pl.program_id(0) == 0)
    def _():
        for c in range(halves):
            columns = [head_rows(grads_ref, c, h, copies, blk) for h in range(heads)]
            for part in range(3):
                rows_ref[c, :, part * heads * HD : (part + 1) * heads * HD] = jnp.concatenate(
                    [column[part * HD : (part + 1) * HD] for column in columns], axis=0
                ).T

    for c in range(halves):
        out_ref[c] = dot(rows_ref[c], weight_ref[...], 1, 1).astype(bf16)


def project_back(blk, grads, weight):
    devices, halves, _, ch = grads.shape
    width, total = weight.shape
    block = min(512, width)
    return pl.pallas_call(
        functools.partial(project_back_kernel, heads=total // (3 * HD)),
        grid=(width // block,),
        in_specs=[
            smem,
            whole(grads.shape),
            pl.BlockSpec((block, total), lambda step: (step, 0)),
        ],
        out_specs=[
            pl.BlockSpec((halves, ch, block), lambda step: (0, 0, step)),
            whole((halves, ch, total)),
        ],
        out_shape=[
            jax.ShapeDtypeStruct((halves, ch, width), bf16),
            jax.ShapeDtypeStruct((halves, ch, total), bf16),
        ],
        compiler_params=compiler_params(32),
        cost_estimate=pl.CostEstimate(
            flops=2 * halves * ch * width * total,
            bytes_accessed=2 * (grads.size + weight.size + halves * ch * (width + total)),
            transcendentals=0,
        ),
    )(blk, grads, weight)


def attend_kernel(
    place_ref, tiles_ref, along_ref, down_ref, qkv_ref, out_ref, exact_ref, lse_ref, keys, queries, values
):
    blocks, _, ch = qkv_ref.shape
    span = 2 * ch
    tiles = blocks // 2
    mine = tiles_ref.shape[0]
    if mine < tiles:
        out_ref[...] = jnp.zeros(out_ref.shape, out_ref.dtype)
        exact_ref[...] = jnp.zeros(exact_ref.shape, exact_ref.dtype)
        lse_ref[...] = jnp.zeros(lse_ref.shape, lse_ref.dtype)

    def arrange(t, unused):
        for half in range(2):
            block = qkv_ref[place_ref[2 * t + half]]
            columns = slice(half * ch, (half + 1) * ch)
            queries[t, :, columns] = block[:HD]
            keys[t, columns, :] = block[HD : 2 * HD].T
            values[t, :, columns] = block[2 * HD :]
        return unused

    lax.fori_loop(0, tiles, arrange, 0)
    scale = log2_e * HD**-0.5

    def query_tile(step, unused):
        t = tiles_ref[step]
        query = queries[t]

        def visit(j, carry, diagonal=False):
            peak, total, acc = carry
            scores = dot(keys[j], query, 1, 0) * scale
            if diagonal:
                scores = jnp.where(down_ref[...] <= along_ref[...], scores, masked_value)
            new_peak = jnp.maximum(peak, jnp.max(scores, axis=0, keepdims=True))
            weights = jnp.exp2(scores - new_peak)
            shrink = jnp.exp2(peak - new_peak)
            total = total * shrink + jnp.sum(weights, axis=0, keepdims=True)
            acc = acc * shrink + dot(values[j], weights.astype(bf16), 1, 0)
            return new_peak, total, acc

        carry = (
            jnp.full((1, span), masked_value, f32),
            jnp.zeros((1, span), f32),
            jnp.zeros((HD, span), f32),
        )
        carry = visit(t, carry, True)
        peak, total, acc = lax.fori_loop(0, t, visit, carry)
        result = acc / total
        lse = peak + jnp.log2(total)
        for half in range(2):
            at = place_ref[2 * t + half]
            columns = slice(half * ch, (half + 1) * ch)
            exact_ref[at] = result[:, columns]
            out_ref[at] = result[:, columns].astype(bf16)
            lse_ref[at] = lse[:, columns]
        return unused

    lax.fori_loop(0, mine, query_tile, 0)


vmem = pl.BlockSpec(memory_space=pltpu.VMEM)


def attend(place, tiles, along, down, qkv):
    blocks, _, ch = qkv.shape
    n = blocks // 2
    return pl.pallas_call(
        attend_kernel,
        in_specs=[smem, smem] + [vmem] * 3,
        out_specs=[vmem] * 3,
        out_shape=[
            jax.ShapeDtypeStruct((blocks, HD, ch), bf16),
            jax.ShapeDtypeStruct((blocks, HD, ch), f32),
            jax.ShapeDtypeStruct((blocks, 1, ch), f32),
        ],
        scratch_shapes=[
            pltpu.VMEM((n, 2 * ch, HD), bf16),
            pltpu.VMEM((n, HD, 2 * ch), bf16),
            pltpu.VMEM((n, HD, 2 * ch), bf16),
        ],
        compiler_params=compiler_params(40),
        cost_estimate=pl.CostEstimate(
            flops=blocks * blocks * ch * ch * HD * 8,
            bytes_accessed=blocks * ch * HD * 12,
            transcendentals=blocks * blocks * ch * ch // 2,
        ),
    )(place, tiles, along, down, qkv)


def unrotate(values, cosine, sine):
    half = ROT // 2
    first, second = values[:half], values[half:ROT]
    return jnp.concatenate(
        [first * cosine + second * sine, second * cosine - first * sine, values[ROT:]], axis=0
    )


def attend_back_kernel(
    place_ref,
    tiles_ref,
    along_ref,
    down_ref,
    qkv_ref,
    grad_ref,
    exact_ref,
    lse_ref,
    cos_ref,
    sin_ref,
    out_ref,
    sums_ref,
    keys_t,
    keys,
    queries_t,
    queries,
    values,
    grads_t,
    grads,
    lse,
    delta,
    grad_q,
    grad_k,
    grad_v,
):
    blocks, _, ch = qkv_ref.shape
    span = 2 * ch
    tiles = blocks // 2
    mine = tiles_ref.shape[0]

    def arrange(t, unused):
        for half in range(2):
            at = place_ref[2 * t + half]
            block = qkv_ref[at]
            columns = slice(half * ch, (half + 1) * ch)
            queries_t[t, :, columns] = block[:HD]
            queries[t, columns, :] = block[:HD].T
            keys_t[t, :, columns] = block[HD : 2 * HD]
            keys[t, columns, :] = block[HD : 2 * HD].T
            values[t, columns, :] = block[2 * HD :].T
            grad = grad_ref[at]
            grads_t[t, :, columns] = grad
            grads[t, columns, :] = grad.T
            lse[t, :, columns] = lse_ref[at]
            delta[t, :, columns] = jnp.sum(grad.astype(f32) * exact_ref[at], axis=0, keepdims=True)
        grad_q[t] = jnp.zeros(grad_q.shape[1:], f32)
        grad_k[t] = jnp.zeros(grad_k.shape[1:], f32)
        grad_v[t] = jnp.zeros(grad_v.shape[1:], f32)
        return unused

    lax.fori_loop(0, tiles, arrange, 0)
    factor = HD**-0.5
    scale = log2_e * factor

    def query_tile(step, unused):
        t = tiles_ref[step]

        def visit(j, acc, diagonal=False):
            scores = dot(keys[j], queries_t[t], 1, 0) * scale
            weights = jnp.exp2(scores - lse[t])
            if diagonal:
                weights = jnp.where(down_ref[...] <= along_ref[...], weights, 0.0)
            grad_weights = dot(values[j], grads_t[t], 1, 0)
            grad_scores = (weights * (grad_weights - delta[t])).astype(bf16)
            grad_v[j] += dot(weights.astype(bf16), grads[t], 1, 0)
            grad_k[j] += dot(grad_scores, queries[t], 1, 0)
            return acc + dot(keys_t[j], grad_scores, 1, 0)

        acc = visit(t, jnp.zeros((HD, span), f32), True)
        grad_q[t] = lax.fori_loop(0, t, visit, acc)
        return unused

    lax.fori_loop(0, mine, query_tile, 0)

    def finish(t, sums):
        key_t = grad_k[t].T
        value_t = grad_v[t].T
        for half in range(2):
            at = place_ref[2 * t + half]
            columns = slice(half * ch, (half + 1) * ch)
            cosine, sine = cos_ref[2 * t + half], sin_ref[2 * t + half]
            parts = (
                unrotate(grad_q[t][:, columns] * factor, cosine, sine),
                unrotate(key_t[:, columns] * factor, cosine, sine),
                value_t[:, columns],
            )
            rows = jnp.concatenate(parts, axis=0).astype(bf16)
            out_ref[at] = rows
            sums = sums + rows.astype(f32)
        return sums

    sums = lax.fori_loop(0, tiles, finish, jnp.zeros((3 * HD, ch), f32))
    sums_ref[...] = jnp.sum(sums, axis=1, keepdims=True)


def attend_back(place, tiles, along, down, qkv, grad, exact, lse, cosine, sine):
    blocks, _, ch = qkv.shape
    n = blocks // 2
    flat = pltpu.VMEM((n, HD, 2 * ch), bf16)
    tall = pltpu.VMEM((n, 2 * ch, HD), bf16)
    line = pltpu.VMEM((n, 1, 2 * ch), f32)
    return pl.pallas_call(
        attend_back_kernel,
        in_specs=[smem, smem] + [vmem] * 8,
        out_specs=[vmem] * 2,
        out_shape=[
            jax.ShapeDtypeStruct((blocks, 3 * HD, ch), bf16),
            jax.ShapeDtypeStruct((3 * HD, 1), f32),
        ],
        scratch_shapes=[
            flat,
            tall,
            flat,
            tall,
            tall,
            flat,
            tall,
            line,
            line,
            pltpu.VMEM((n, HD, 2 * ch), f32),
            pltpu.VMEM((n, 2 * ch, HD), f32),
            pltpu.VMEM((n, 2 * ch, HD), f32),
        ],
        compiler_params=compiler_params(48),
        cost_estimate=pl.CostEstimate(
            flops=blocks * blocks * ch * ch * HD * 20,
            bytes_accessed=blocks * ch * HD * 24,
            transcendentals=blocks * blocks * ch * ch // 2,
        ),
    )(place, tiles, along, down, qkv, grad, exact, lse, cosine, sine)


def local(
    layer_input,
    block_order,
    first_gain,
    first_shift,
    query_weight,
    key_weight,
    value_weight,
    query_bias,
    key_bias,
    value_bias,
    out_weight,
    second_gain,
    second_shift,
    gate_weight,
    up_weight,
    down_weight,
    out_grad,
):
    seqs, _, halves, part_rows, width = layer_input.shape
    planes = lax.axis_size("plane")
    devices = 2 * planes
    head_size = lax.axis_size("head")
    blk = lax.axis_index("plane") * 2 + lax.axis_index("core")
    head_index = lax.axis_index("head")
    blk_scalar = blk.astype(jnp.int32).reshape(1)
    ch = part_rows * head_size
    blocks = halves * devices
    heads = query_bias.shape[0]
    local_width = heads * HD
    copies = devices // heads

    part = first_gain.shape[0]
    q_dims, k_dims = query_bias.shape[1], key_bias.shape[1]
    small = jnp.concatenate(
        [first_gain, first_shift, second_gain, second_shift]
        + [member.reshape(-1) for member in (query_bias, key_bias, value_bias)]
    )

    owner = jnp.arange(devices, dtype=jnp.int32) ^ blk
    first_id = block_order[owner]
    rank = jnp.stack([first_id, 2 * devices - 1 - first_id], axis=1).reshape(-1)
    place = jnp.zeros((blocks,), jnp.int32).at[rank].set(jnp.arange(blocks, dtype=jnp.int32))
    offsets = head_offsets(part_rows)
    own_positions = rank[:halves, None] * ch + offsets[None, :]
    cos_own, sin_own = rotary_tables(own_positions)
    all_positions = jnp.arange(blocks, dtype=jnp.int32)[:, None] * ch + offsets[None, :]
    cos_all, sin_all = rotary_tables(all_positions)
    along = all_positions[:2].reshape(1, -1)
    down = all_positions[:2].reshape(-1, 1)
    tile_count = blocks // 2
    cycle = jnp.arange(tile_count // copies, dtype=jnp.int32)
    share = blk % copies
    tiles = (cycle // 2) * 2 * copies + jnp.where(cycle % 2 == 0, share, 2 * copies - 1 - share)
    if copies == 1:
        tiles = jnp.arange(tile_count, dtype=jnp.int32)

    full_qkv = blk_gather(jnp.concatenate([query_weight, key_weight, value_weight], axis=1))
    full_out = blk_gather(out_weight, 1)

    def split_small(small):
        small = small_gather(in_head_order(small[0], 0), BLK).astype(f32)
        gain_one, shift_one, gain_two, shift_two = [
            small[:, k * part : (k + 1) * part].reshape(-1) for k in range(4)
        ]
        biases = lax.dynamic_index_in_dim(
            small[:, 4 * part :].reshape(devices, head_size, -1), head_index, 1, keepdims=False
        )

        def bias_of(start, dims):
            member = biases[:, start : start + heads * dims].reshape(devices, heads, dims)
            return jnp.swapaxes(member, 0, 1).reshape(heads, devices * dims)

        bias_query = bias_of(0, q_dims)
        bias_key = jnp.pad(bias_of(heads * q_dims, k_dims), ((0, 0), (0, HD - ROT)))
        bias_value = bias_of(heads * (q_dims + k_dims), q_dims)
        bias = jnp.concatenate([bias_query, bias_key, bias_value], axis=0).reshape(1, -1)
        return gain_one, shift_one, gain_two, shift_two, bias

    each = range(seqs)
    inputs = [layer_input[s, 0] for s in each]
    grad_own = [out_grad[s, 0] for s in each]
    rows_in = [member.astype(f32) for member in inputs]

    def norm_one(whole_rows):
        return normalize(whole_rows.astype(f32), gain_one, shift_one).astype(bf16)

    def norm_one_sums(whole_rows, summand):
        value = whole_rows.astype(f32)
        upstream = summand.astype(f32)
        center = value - jnp.mean(value, axis=-1, keepdims=True)
        inverse = lax.rsqrt(jnp.mean(center * center, axis=-1, keepdims=True) + epsilon)
        return jnp.sum(upstream * (center * inverse), axis=(0, 1)), jnp.sum(upstream, axis=(0, 1))

    def queries_of(rows):
        return project_in(blk_scalar, rows, full_qkv, bias, cos_own, sin_own, devices)

    def move(value, rows):
        return exchange(value.reshape(devices, halves, rows, ch))

    def norm_two(value):
        return normalize(value, gain_two, shift_two).astype(bf16)

    def flat(member):
        return member.reshape(-1, member.shape[-1])

    def feed_first(rows, grad):
        gate = dot(flat(rows), full_gate, 1, 0)
        up_value = dot(flat(rows), full_up, 1, 0)
        sigmoid_gate = jax.nn.sigmoid(gate)
        silu_gate = gate * sigmoid_gate
        hidden = (silu_gate * up_value).astype(bf16)
        grad_hidden = dot(flat(grad), full_down, 1, 1)
        grad_up = (grad_hidden * silu_gate).astype(bf16)
        grad_gate = (
            grad_hidden * up_value * sigmoid_gate * (1.0 + gate * (1.0 - sigmoid_gate))
        ).astype(bf16)
        return hidden, grad_gate, grad_up

    def feed_back(grad_gate, grad_up):
        summand = dot(grad_gate, full_gate, 1, 1) + dot(grad_up, full_up, 1, 1)
        return summand.astype(bf16).reshape(halves, ch, width)

    def feed_out(hidden):
        return dot(hidden, full_down, 1, 0).astype(bf16).reshape(halves, ch, width)

    def back_two(s, parts, middle):
        back, gain_grad, shift_grad = norm_back(middle, gain_two, scatter_whole(parts))
        grad = grad_own[s].astype(f32) + back
        return grad, grad.astype(bf16), (gain_grad, shift_grad)

    def back_one(s, parts, grad_middle):
        back, _, _ = norm_back(rows_in[s], gain_one, scatter_whole(parts))
        return grad_middle + back

    def attend_of(qkv):
        return attend(place, tiles, along, down, qkv.reshape(blocks, 3 * HD, ch))

    def attend_back_of(qkv, attended, grad):
        _, exact, lse = attended
        grad = grad.reshape(blocks, HD, ch)
        qkv = qkv.reshape(blocks, 3 * HD, ch)
        return attend_back(place, tiles, along, down, qkv, grad, exact, lse, cos_all, sin_all)

    def weight_grad(lefts, rights):
        total = dot(flat(lefts[0]), flat(rights[0]), 0, 0)
        for left, right in zip(lefts[1:], rights[1:]):
            total = total + dot(flat(left), flat(right), 0, 0)
        return total.astype(bf16)

    stage = lax.optimization_barrier
    in_a, in_b = inputs
    small = small[None, None]
    got, got_small = gather_first(in_a), gather_first(small)
    in_a, small, got, got_small, in_b = stage((in_a, small, got, got_small, in_b))
    parts, small = gather_rest(in_a, got), gather_rest(small, got_small)
    parts, small, in_b = stage((parts, small, in_b))
    got = gather_first(in_b)
    x_a = gather_whole(parts)
    gain_one, shift_one, gain_two, shift_two, bias = split_small(gather_whole(small))
    one_a = norm_one(x_a)
    qkv_a = queries_of(one_a)
    got, in_b, x_a, one_a, qkv_a, own_grads = stage((got, in_b, x_a, one_a, qkv_a, out_grad))
    grads = lax.all_gather(own_grads[:, 0], "head", axis=2, tiled=True)
    parts = gather_rest(in_b, got)
    qkv_a = move(qkv_a, 3 * HD)
    parts, qkv_a, late = stage((parts, qkv_a, (gate_weight, up_weight, down_weight)))
    full_gate, full_up, full_down = blk_gather(late[0]), blk_gather(late[1]), blk_gather(late[2], 1)
    x_b = gather_whole(parts)
    one_b = norm_one(x_b)
    qkv_b = move(queries_of(one_b), 3 * HD)
    att_a = attend_of(qkv_a)
    x_b, one_b, qkv_b, att_a = stage((x_b, one_b, qkv_b, att_a))
    att = move(att_a[0], HD)
    att, qkv_b = stage((att, qkv_b))
    partial, out_a = project_out(blk_scalar, att, full_out)
    sums = scatter_first(partial)
    att_b = attend_of(qkv_b)
    sums, att_b, out_a = stage((sums, att_b, out_a))
    sums = scatter_rest(sums)
    att = move(att_b[0], HD)
    partial, out_b = project_out(blk_scalar, att, full_out)
    sums, partial, out_b = stage((sums, partial, out_b))
    middle_a = rows_in[0] + scatter_whole(sums)
    normed = norm_two(middle_a)
    got = gather_first(normed)
    sums = scatter_first(partial)
    got, sums, normed, middle_a, grads = stage((got, sums, normed, middle_a, grads))
    parts = gather_rest(normed, got)
    sums = scatter_rest(sums)
    grads = in_head_order(grads, 2)
    parts, sums, (grad_a, grad_b) = stage((parts, sums, (grads[0], grads[1])))
    middle_b = rows_in[1] + scatter_whole(sums)
    normed = norm_two(middle_b)
    got = gather_first(normed)
    two_a = gather_whole(parts)
    hid_a, gate_a, up_a = feed_first(two_a, grad_a)
    got, normed, middle_b, two_a, hid_a, gate_a, up_a = stage(
        (got, normed, middle_b, two_a, hid_a, gate_a, up_a)
    )
    parts = gather_rest(normed, got)
    partial = feed_back(gate_a, up_a)
    parts, partial, hid_a, gate_a, up_a = stage((parts, partial, hid_a, gate_a, up_a))
    sums = scatter_first(partial)
    two_b = gather_whole(parts)
    hid_b, gate_b, up_b = feed_first(two_b, grad_b)
    sums, two_b, hid_b, gate_b, up_b = stage((sums, two_b, hid_b, gate_b, up_b))
    sums = scatter_rest(sums)
    partial = feed_back(gate_b, up_b)
    sums, partial, hid_a, hid_b, gate_b, up_b, two_b = stage(
        (sums, partial, hid_a, hid_b, gate_b, up_b, two_b)
    )
    mid_grad_a, branch_a, norm_grads_two_a = back_two(0, sums, middle_a)
    got = gather_first(branch_a)
    sums = scatter_first(partial)
    down_grad = weight_grad((hid_a, hid_b), (grad_a, grad_b))
    feeds = jnp.concatenate([feed_out(hid_a), feed_out(hid_b)])
    got, sums, down_grad, feeds, branch_a, mid_grad_a, gate_a, up_a = stage(
        (got, sums, down_grad, feeds, branch_a, mid_grad_a, gate_a, up_a)
    )
    down_grad = blk_scatter(down_grad, 1)
    parts = gather_rest(branch_a, got)
    sums = scatter_rest(sums)
    gate_grad = weight_grad((two_a, two_b), (gate_a, gate_b))
    up_grad = weight_grad((two_a, two_b), (up_a, up_b))
    parts, sums, gate_grad, up_grad, feeds = stage((parts, sums, gate_grad, up_grad, feeds))
    gate_grad = blk_scatter(gate_grad)
    up_grad = blk_scatter(up_grad)
    mid_grad_b, branch_b, norm_grads_two_b = back_two(1, sums, middle_b)
    got = gather_first(branch_b)
    whole_a = gather_whole(parts)
    att_grad_a = move(project_grad(blk_scalar, whole_a, full_out, devices), HD)
    got, branch_b, mid_grad_b, whole_a, att_grad_a, feeds = stage(
        (got, branch_b, mid_grad_b, whole_a, att_grad_a, feeds)
    )
    parts = gather_rest(branch_b, got)
    feeds = scatter_first(feeds)
    made_a, bias_sums_a = attend_back_of(qkv_a, att_a, att_grad_a)
    parts, feeds, made_a, whole_a = stage((parts, feeds, made_a, whole_a))
    whole_b = gather_whole(parts)
    att_grad_b = move(project_grad(blk_scalar, whole_b, full_out, devices), HD)
    out_weight_grad = weight_grad((out_a, out_b), (whole_a, whole_b))
    feeds, made_a, att_grad_b, out_weight_grad, down_grad = stage(
        (feeds, made_a, att_grad_b, out_weight_grad, down_grad)
    )
    out_weight_grad = blk_scatter(out_weight_grad, 1)
    feeds = scatter_rest(feeds)
    moved = move(made_a, 3 * HD)
    made_b, bias_sums_b = attend_back_of(qkv_b, att_b, att_grad_b)
    feeds, moved, made_b = stage((feeds, moved, made_b))
    partial_a, qkv_rows_a = project_back(blk_scalar, moved, full_qkv)
    sums = scatter_first(partial_a)
    moved = move(made_b, 3 * HD)
    feeds = scatter_whole(feeds)
    layer_output = (middle_a + feeds[:halves], middle_b + feeds[halves:])
    sums, moved, partial_a, qkv_rows_a, layer_output, gate_grad = stage(
        (sums, moved, partial_a, qkv_rows_a, layer_output, gate_grad)
    )
    partial_b, qkv_rows_b = project_back(blk_scalar, moved, full_qkv)
    sums_b = scatter_first(partial_b)
    sums = scatter_rest(sums)
    qkv_grad = weight_grad((one_a, one_b), (qkv_rows_a, qkv_rows_b))
    norm_grads_one_a = norm_one_sums(x_a, partial_a)
    sums, sums_b, partial_b, qkv_grad, norm_grads_one_a = stage(
        (sums, sums_b, partial_b, qkv_grad, norm_grads_one_a)
    )
    qkv_grad = blk_scatter(qkv_grad)
    sums_b = scatter_rest(sums_b)
    norm_grads_one_b = norm_one_sums(x_b, partial_b)
    input_grad = (back_one(0, sums, mid_grad_a), back_one(1, sums_b, mid_grad_b))
    norm_one_grads = (norm_grads_one_a, norm_grads_one_b)
    norm_two_grads = (norm_grads_two_a, norm_grads_two_b)
    bias_sums = (bias_sums_a, bias_sums_b)

    def over_all(grads, k):
        total = grads[0][k]
        for s in range(1, seqs):
            total = total + grads[s][k]
        return total.reshape(devices * head_size, part)

    bias_total = bias_sums[0]
    for s in range(1, seqs):
        bias_total = bias_total + bias_sums[s]
    bias_total = bias_total.reshape(3, HD)
    shares = jnp.concatenate(
        [
            bias_total[0].reshape(devices, q_dims),
            bias_total[1, :ROT].reshape(devices, k_dims),
            bias_total[2].reshape(devices, q_dims),
        ],
        axis=1,
    )
    own_head = (jnp.arange(heads, dtype=jnp.int32) == blk // copies).astype(f32)
    own_column = (jnp.arange(head_size, dtype=jnp.int32) == head_index).astype(f32)
    spread = (
        shares[:, None, None, :] * own_head[None, None, :, None] * own_column[None, :, None, None]
    ).reshape(devices * head_size, -1)
    smalls = jnp.concatenate(
        [
            over_all(norm_one_grads, 0),
            over_all(norm_one_grads, 1),
            over_all(norm_two_grads, 0),
            over_all(norm_two_grads, 1),
            spread,
        ],
        axis=1,
    )
    smalls = small_scatter(smalls)
    norm_grads = [smalls[k * part : (k + 1) * part] for k in range(4)]
    bias_grads = smalls[4 * part :].reshape(heads, 2 * q_dims + k_dims)
    stacked = lambda members: jnp.stack(members)[:, None]
    return (
        stacked(layer_output),
        stacked(input_grad),
        norm_grads[0],
        norm_grads[1],
        qkv_grad[:, :local_width],
        qkv_grad[:, local_width : 2 * local_width],
        qkv_grad[:, 2 * local_width :],
        bias_grads[:, :q_dims],
        bias_grads[:, q_dims : q_dims + k_dims],
        bias_grads[:, q_dims + k_dims :],
        out_weight_grad,
        norm_grads[2],
        norm_grads[3],
        gate_grad,
        up_grad,
        down_grad,
    )


def solution(mesh):
    blk_size, head_size = mesh.devices.shape
    split = Mesh(mesh.devices.reshape(blk_size // 2, 2, head_size), ALL)
    tokens = P(None, BLK, None, "head", None)
    rows = P(BLK, "head")
    columns = P("head", BLK)
    return jax.shard_map(
        local,
        mesh=split,
        in_specs=(
            tokens,
            P(),
            P(ALL),
            P(ALL),
            rows,
            rows,
            rows,
            columns,
            columns,
            columns,
            columns,
            P(ALL),
            P(ALL),
            rows,
            rows,
            columns,
            tokens,
        ),
        out_specs=(
            tokens,
            tokens,
            P(ALL),
            P(ALL),
            rows,
            rows,
            rows,
            columns,
            columns,
            columns,
            columns,
            P(ALL),
            P(ALL),
            rows,
            rows,
            columns,
        ),
        check_vma=False,
    )
```

```python
import functools
import math

import jax
import jax.numpy as jnp
from jax import lax
from jax.experimental import pallas as pl
from jax.experimental.pallas import tpu as pltpu
from jax.sharding import Mesh
from jax.sharding import PartitionSpec as P

HD = 64
ROT = 16

epsilon = 1e-05
masked_value = -1e30
rotary_base = 10000.0
log2_e = math.log2(math.e)
f32 = jnp.float32
bf16 = jnp.bfloat16
BLK = ("plane", "core")
ALL = ("plane", "core", "head")
MIB = 2**20


def dot(left, right, left_axis, right_axis):
    return lax.dot_general(
        left, right, (((left_axis,), (right_axis,)), ((), ())), preferred_element_type=f32
    )


def paired(value, axis, step):
    count = lax.axis_size(axis)
    return lax.ppermute(value, axis, [(source, source ^ step) for source in range(count)])


def exchange_first(value):
    planes = lax.axis_size("plane")
    value = value.reshape((planes, 2) + value.shape[1:])
    return value[:, 0], paired(value[:, 1], "core", 1)


def exchange_rest(parts):
    near, crossed = parts
    received = [jnp.stack([near[0], crossed[0]])]
    for step in range(1, near.shape[0]):
        received.append(paired(jnp.stack([near[step], crossed[step]]), "plane", step))
    received = jnp.stack(received)
    return received.reshape((-1,) + received.shape[2:])


def steps_of(axes):
    for axis in reversed(axes):
        step = 1
        while step < lax.axis_size(axis):
            yield axis, step
            step *= 2


def small_gather(value, axes):
    for axis, step in steps_of(axes):
        other = paired(value, axis, step)
        low = (lax.axis_index(axis) & step) == 0
        value = jnp.concatenate([jnp.where(low, value, other), jnp.where(low, other, value)])
    return value


def small_scatter(value, axes):
    shape = value.shape[1:]
    for axis, step in steps_of(axes):
        value = value.reshape((-1, 2) + shape)
        low = (lax.axis_index(axis) & step) == 0
        keep = jnp.where(low, value[:, 0], value[:, 1])
        value = keep + paired(jnp.where(low, value[:, 1], value[:, 0]), axis, step)
    return value.reshape(shape)


def in_chain():
    return lax.axis_size("head") == 4


def head_order():
    first = lax.axis_index("head") if in_chain() else 0
    return first ^ jnp.arange(lax.axis_size("head"), dtype=jnp.int32)


def head_offsets(part_rows):
    inner = jnp.arange(part_rows, dtype=jnp.int32)
    return (head_order()[:, None] * part_rows + inner[None, :]).reshape(-1)


def in_head_order(value, axis):
    if not in_chain():
        return value
    order = head_order()
    rows = value.shape[axis] // lax.axis_size("head")
    return jnp.concatenate(
        [
            lax.dynamic_slice_in_dim(value, order[k] * rows, rows, axis)
            for k in range(lax.axis_size("head"))
        ],
        axis=axis,
    )


ONE = [(0, 1), (1, 0), (2, 3), (3, 2)]
TWO = [(0, 2), (1, 3), (2, 0), (3, 1)]
THREE = [(0, 3), (1, 2), (2, 1), (3, 0)]
MIDDLE = [(1, 2), (2, 1)]
OUTWARD = [(1, 0), (2, 3)]
INWARD = [(0, 1), (3, 2)]


def gather_first(value):
    if not in_chain():
        return value
    return lax.ppermute(value, "head", TWO), lax.ppermute(value, "head", ONE)


def gather_rest(value, received):
    if not in_chain():
        return lax.all_gather(value, "head", axis=1, tiled=True)
    two, one = received
    return (
        value,
        one,
        two,
        lax.ppermute(two, "head", OUTWARD),
        lax.ppermute(value, "head", MIDDLE),
    )


def gather_direct(value):
    if not in_chain():
        return lax.all_gather(value, "head", axis=1, tiled=True)
    two = lax.ppermute(value, "head", TWO)
    three = lax.ppermute(value, "head", THREE)
    return value, lax.ppermute(value, "head", ONE), two, three, three


def gather_pieces(parts):
    return parts if in_chain() else (parts,)


def gather_whole(parts):
    if not in_chain():
        return parts
    value, one, two, far, near = parts
    last = jnp.where(ends_chain() == 1, far, near)
    return jnp.concatenate([value, one, two, last], axis=1)


def ends_chain():
    index = lax.axis_index("head")
    return ((index == 0) | (index == lax.axis_size("head") - 1)).astype(jnp.int32)


def scatter_first(pieces):
    if not in_chain():
        return pieces[0]
    own, one, two, last = pieces
    far = lax.ppermute(last, "head", INWARD)
    return scatter_pass((own, one, two, far, lax.ppermute(last, "head", MIDDLE)))


def scatter_pass(parts):
    if not in_chain():
        return parts
    own, one, two, far, near = parts
    return own, one, (two.astype(f32) + far.astype(f32)).astype(bf16), near


def scatter_rest(parts):
    if not in_chain():
        return lax.psum_scatter(parts, "head", scatter_dimension=1, tiled=True)
    own, one, passed, near = parts
    return own, lax.ppermute(passed, "head", TWO), lax.ppermute(one, "head", ONE), near


def scatter_pieces(parts):
    return parts if in_chain() else (parts,)


def scatter_whole(parts):
    total = [member.astype(f32) for member in scatter_pieces(parts)]
    return functools.reduce(jnp.add, total)


def blk_gather(value, axis=0):
    return lax.all_gather(value, BLK, axis=axis, tiled=True)


def blk_scatter(value, axis=0):
    return lax.psum_scatter(value, BLK, scatter_dimension=axis, tiled=True)


def rotary_tables(positions):
    frequency = jnp.exp(
        jnp.arange(ROT // 2, dtype=jnp.float32) * (-2.0 * math.log(rotary_base) / ROT)
    )
    phase_angle = positions.astype(f32)[:, None, :] * frequency[None, :, None]
    return (jnp.cos(phase_angle), jnp.sin(phase_angle))


smem = pl.BlockSpec(memory_space=pltpu.SMEM)
vmem = pl.BlockSpec(memory_space=pltpu.VMEM)


def whole(shape):
    return pl.BlockSpec(shape, lambda step: (0,) * len(shape))


light = pl.CostEstimate(flops=1000, bytes_accessed=1000, transcendentals=0)
heavy = pl.CostEstimate(flops=30 * 10**9, bytes_accessed=1000, transcendentals=0)


def compiler_params(mebibytes):
    return pltpu.CompilerParams(vmem_limit_bytes=mebibytes * MIB)


def piece(refs, k, c, ends):
    if k < 3:
        return refs[k][c]
    return jnp.where(ends == 1, refs[3][c], refs[4][c])


def each_piece(refs):
    count = 4 if len(refs) == 5 else 1
    return [(k, slice(k * refs[0].shape[1], (k + 1) * refs[0].shape[1])) for k in range(count)]


def row_norm(value):
    center = value - jnp.mean(value, axis=-1, keepdims=True)
    inverse = lax.rsqrt(jnp.mean(center * center, axis=-1, keepdims=True) + epsilon)
    return center * inverse, inverse


def project_in_kernel(blk_ref, *refs, pieces):
    rows_in = refs[:pieces]
    gain_ref, shift_ref, query_ref, key_ref, value_ref, bias_q, bias_k, bias_v = refs[
        pieces : pieces + 8
    ]
    cos_ref, sin_ref, out_ref, rows_ref = refs[pieces + 8 :]
    group = pl.program_id(0)
    blk = blk_ref[0]
    halves = rows_ref.shape[0]
    heads = query_ref.shape[1] // HD
    copies = out_ref.shape[0] // (heads * pl.num_programs(0))
    half = ROT // 2

    @pl.when(group == 0)
    def _():
        for c in range(halves):
            for k, place in each_piece(rows_in):
                normed, _ = row_norm(piece(rows_in, k, c, blk_ref[1]).astype(f32))
                rows_ref[c, place, :] = (normed * gain_ref[...] + shift_ref[...]).astype(bf16)

    for part, (weight, bias) in enumerate(
        ((query_ref, bias_q), (key_ref, bias_k), (value_ref, bias_v))
    ):
        for c in range(halves):
            result = dot(rows_ref[c], weight[...], 1, 0) + bias[...]
            result = result.T
            cosine, sine = cos_ref[c], sin_ref[c]
            for h in range(heads):
                values = result[h * HD : (h + 1) * HD]
                if part < 2:
                    first, second = values[:half], values[half:ROT]
                    values = jnp.concatenate(
                        [
                            first * cosine - second * sine,
                            second * cosine + first * sine,
                            values[ROT:],
                        ],
                        axis=0,
                    )
                values = values.astype(bf16)
                for copy in range(copies):
                    at = ((group * heads + h) * copies + copy) ^ blk
                    out_ref[at, c, part * HD : (part + 1) * HD, :] = values


def project_in(blk, pieces, gain, shift, weight, bias, cosine, sine, devices):
    halves, _, width = pieces[0].shape
    ch = cosine.shape[-1]
    total = weight.shape[1] // 3
    block = min(4 * HD, total)
    groups = total // block
    weights = [
        pl.BlockSpec((width, block), functools.partial(lambda p, g: (0, p * groups + g), part))
        for part in range(3)
    ]
    biases = [
        pl.BlockSpec((1, block), functools.partial(lambda p, g: (0, p * groups + g), part))
        for part in range(3)
    ]
    out = (devices, halves, 3 * HD, ch)
    rows = (halves, ch, width)
    return pl.pallas_call(
        functools.partial(project_in_kernel, pieces=len(pieces)),
        grid=(groups,),
        in_specs=[smem]
        + [whole(member.shape) for member in pieces]
        + [whole(gain.shape)] * 2
        + weights
        + biases
        + [whole(cosine.shape), whole(sine.shape)],
        out_specs=[whole(out), whole(rows)],
        out_shape=[jax.ShapeDtypeStruct(out, bf16), jax.ShapeDtypeStruct(rows, bf16)],
        compiler_params=compiler_params(48),
        cost_estimate=light,
    )(blk, *pieces, gain, shift, weight, weight, weight, bias, bias, bias, cosine, sine)


def add_all(refs, c):
    total = refs[0][c].astype(f32)
    for ref in refs[1:]:
        total = total + ref[c].astype(f32)
    return total


def middle_kernel(*refs):
    sums = refs[:-5]
    rows_ref, gain_ref, shift_ref, middle_ref, normed_ref = refs[-5:]
    for c in range(rows_ref.shape[0]):
        value = rows_ref[c].astype(f32) + add_all(sums, c)
        middle_ref[c] = value
        normed, _ = row_norm(value)
        normed_ref[c] = (normed * gain_ref[...] + shift_ref[...]).astype(bf16)


def middle_of(sums, rows, gain, shift):
    return pl.pallas_call(
        middle_kernel,
        in_specs=[vmem] * (len(sums) + 3),
        out_specs=[vmem] * 2,
        out_shape=[
            jax.ShapeDtypeStruct(rows.shape, f32),
            jax.ShapeDtypeStruct(rows.shape, bf16),
        ],
        compiler_params=compiler_params(32),
        cost_estimate=light,
    )(*sums, rows, gain, shift)


def norm_back_rows(value, gain, upstream):
    normed, inverse = row_norm(value)
    scaled = upstream * gain
    back = inverse * (
        scaled
        - jnp.mean(scaled, axis=-1, keepdims=True)
        - normed * jnp.mean(scaled * normed, axis=-1, keepdims=True)
    )
    return back, normed


def back_two_kernel(*refs):
    sums = refs[:-7]
    middle_ref, grad_ref, gain_ref, out_ref, low_ref, gain_sum, shift_sum = refs[-7:]
    gain_total = shift_total = 0.0
    for c in range(middle_ref.shape[0]):
        upstream = add_all(sums, c)
        back, normed = norm_back_rows(middle_ref[c], gain_ref[...], upstream)
        grad = grad_ref[c].astype(f32) + back
        out_ref[c] = grad
        low_ref[c] = grad.astype(bf16)
        gain_total = gain_total + jnp.sum(upstream * normed, axis=0, keepdims=True)
        shift_total = shift_total + jnp.sum(upstream, axis=0, keepdims=True)
    gain_sum[...] = gain_total
    shift_sum[...] = shift_total


def back_two(sums, middle, grad, gain):
    line = jax.ShapeDtypeStruct(gain.shape, f32)
    return pl.pallas_call(
        back_two_kernel,
        in_specs=[vmem] * (len(sums) + 3),
        out_specs=[vmem] * 4,
        out_shape=[
            jax.ShapeDtypeStruct(middle.shape, f32),
            jax.ShapeDtypeStruct(middle.shape, bf16),
            line,
            line,
        ],
        compiler_params=compiler_params(32),
        cost_estimate=light,
    )(*sums, middle, grad, gain)


def back_one_kernel(*refs):
    sums = refs[:-4]
    rows_ref, grad_ref, gain_ref, out_ref = refs[-4:]
    for c in range(rows_ref.shape[0]):
        back, _ = norm_back_rows(rows_ref[c].astype(f32), gain_ref[...], add_all(sums, c))
        out_ref[c] = grad_ref[c] + back


def back_one(sums, rows, grad, gain):
    return pl.pallas_call(
        back_one_kernel,
        in_specs=[vmem] * (len(sums) + 3),
        out_specs=vmem,
        out_shape=jax.ShapeDtypeStruct(rows.shape, f32),
        compiler_params=compiler_params(32),
        cost_estimate=light,
    )(*sums, rows, grad, gain)


def head_rows(ref, c, head, copies, blk):
    values = ref[(head * copies) ^ blk, c]
    if copies == 1:
        return values
    values = values.astype(f32)
    for copy in range(1, copies):
        values = values + ref[(head * copies + copy) ^ blk, c].astype(f32)
    return values.astype(bf16)


def put_pieces(refs, c, rows):
    step = rows.shape[0] // len(refs)
    for k, ref in enumerate(refs):
        ref[c] = rows[k * step : (k + 1) * step]


def project_out_kernel(blk_ref, attended_ref, weight_ref, rows_ref, *out_refs, heads):
    blk = blk_ref[0]
    halves = rows_ref.shape[0]
    copies = attended_ref.shape[0] // heads

    @pl.when(pl.program_id(0) == 0)
    def _():
        for c in range(halves):
            columns = [head_rows(attended_ref, c, h, copies, blk) for h in range(heads)]
            rows_ref[c] = jnp.concatenate(columns, axis=0).T

    for c in range(halves):
        put_pieces(out_refs, c, dot(rows_ref[c], weight_ref[...], 1, 0).astype(bf16))


def project_out(blk, attended, weight, pieces):
    devices, halves, _, ch = attended.shape
    total, width = weight.shape
    block = min(1024, width)
    part = ch // pieces
    rows, *out = pl.pallas_call(
        functools.partial(project_out_kernel, heads=total // HD),
        grid=(width // block,),
        in_specs=[
            smem,
            whole(attended.shape),
            pl.BlockSpec((total, block), lambda step: (0, step)),
        ],
        out_specs=[whole((halves, ch, total))]
        + [pl.BlockSpec((halves, part, block), lambda step: (0, 0, step))] * pieces,
        out_shape=[jax.ShapeDtypeStruct((halves, ch, total), bf16)]
        + [jax.ShapeDtypeStruct((halves, part, width), bf16)] * pieces,
        compiler_params=compiler_params(32),
        cost_estimate=light,
    )(blk, attended, weight)
    return out, rows


def project_grad_kernel(blk_ref, *refs, pieces):
    rows_in = refs[:pieces]
    weight_ref, out_ref, rows_ref = refs[pieces:]
    group = pl.program_id(0)
    blk = blk_ref[0]
    heads = weight_ref.shape[0] // HD
    copies = out_ref.shape[0] // (heads * pl.num_programs(0))

    @pl.when(group == 0)
    def _():
        for c in range(rows_ref.shape[0]):
            for k, place in each_piece(rows_in):
                rows_ref[c, place, :] = piece(rows_in, k, c, blk_ref[1])

    for c in range(rows_ref.shape[0]):
        result = dot(weight_ref[...], rows_ref[c], 1, 1).astype(bf16)
        for h in range(heads):
            for copy in range(copies):
                at = ((group * heads + h) * copies + copy) ^ blk
                out_ref[at, c] = result[h * HD : (h + 1) * HD]


def project_grad(blk, pieces, weight, devices, ch):
    halves, _, width = pieces[0].shape
    total = weight.shape[0]
    block = min(4 * HD, total)
    out = (devices, halves, HD, ch)
    rows = (halves, ch, width)
    return pl.pallas_call(
        functools.partial(project_grad_kernel, pieces=len(pieces)),
        grid=(total // block,),
        in_specs=[smem]
        + [whole(member.shape) for member in pieces]
        + [pl.BlockSpec((block, width), lambda step: (step, 0))],
        out_specs=[whole(out), whole(rows)],
        out_shape=[jax.ShapeDtypeStruct(out, bf16), jax.ShapeDtypeStruct(rows, bf16)],
        compiler_params=compiler_params(32),
        cost_estimate=light,
    )(blk, *pieces, weight)


def project_back_kernel(blk_ref, *refs, pieces, heads):
    rows_in = refs[:pieces]
    grads_ref, weight_ref, rows_ref, gain_sum, shift_sum = refs[pieces : pieces + 5]
    out_refs, (mean_ref, inverse_ref) = refs[pieces + 5 : -2], refs[-2:]
    blk = blk_ref[0]
    step = pl.program_id(0)
    halves, _, block = out_refs[0].shape
    copies = grads_ref.shape[0] // heads

    @pl.when(step == 0)
    def _():
        for c in range(halves):
            columns = [head_rows(grads_ref, c, h, copies, blk) for h in range(heads)]
            for part in range(3):
                rows_ref[c, :, part * heads * HD : (part + 1) * heads * HD] = jnp.concatenate(
                    [column[part * HD : (part + 1) * HD] for column in columns], axis=0
                ).T
            for k, place in each_piece(rows_in):
                value = piece(rows_in, k, c, blk_ref[1]).astype(f32)
                mean = jnp.mean(value, axis=-1, keepdims=True)
                center = value - mean
                mean_ref[c, place, :] = mean
                inverse_ref[c, place, :] = lax.rsqrt(
                    jnp.mean(center * center, axis=-1, keepdims=True) + epsilon
                )

    gain_total = shift_total = 0.0
    columns = pl.ds(pl.multiple_of(step * block, block), block)
    for c in range(halves):
        result = dot(rows_ref[c], weight_ref[...], 1, 1)
        put_pieces(out_refs, c, result.astype(bf16))
        shift_total = shift_total + jnp.sum(result, axis=0, keepdims=True)
        for k, place in each_piece(rows_in):
            if k < 3:
                value = rows_in[k][c, :, columns]
            else:
                value = jnp.where(
                    blk_ref[1] == 1, rows_in[3][c, :, columns], rows_in[4][c, :, columns]
                )
            normed = (value.astype(f32) - mean_ref[c, place, :]) * inverse_ref[c, place, :]
            gain_total = gain_total + jnp.sum(result[place] * normed, axis=0, keepdims=True)
    gain_sum[...] = gain_total
    shift_sum[...] = shift_total


def project_back(blk, pieces, grads, weight, cuts):
    devices, halves, _, ch = grads.shape
    width, total = weight.shape
    block = min(512, width)
    part = ch // cuts
    line = pl.BlockSpec((1, block), lambda step: (0, step))
    rows, gain, shift, *out = pl.pallas_call(
        functools.partial(project_back_kernel, pieces=len(pieces), heads=total // (3 * HD)),
        grid=(width // block,),
        in_specs=[smem]
        + [whole(member.shape) for member in pieces]
        + [whole(grads.shape), pl.BlockSpec((block, total), lambda step: (step, 0))],
        out_specs=[whole((halves, ch, total)), line, line]
        + [pl.BlockSpec((halves, part, block), lambda step: (0, 0, step))] * cuts,
        out_shape=[
            jax.ShapeDtypeStruct((halves, ch, total), bf16),
            jax.ShapeDtypeStruct((1, width), f32),
            jax.ShapeDtypeStruct((1, width), f32),
        ]
        + [jax.ShapeDtypeStruct((halves, part, width), bf16)] * cuts,
        scratch_shapes=[pltpu.VMEM((halves, ch, 1), f32)] * 2,
        compiler_params=compiler_params(40),
        cost_estimate=light,
    )(blk, *pieces, grads, weight)
    return out, rows, gain, shift


def attend_kernel(
    place_ref, tiles_ref, along_ref, down_ref, qkv_ref, out_ref, exact_ref, lse_ref, keys, queries, values
):
    blocks, _, ch = qkv_ref.shape
    span = 2 * ch
    tiles = blocks // 2
    mine = tiles_ref.shape[0]
    if mine < tiles:
        out_ref[...] = jnp.zeros(out_ref.shape, out_ref.dtype)
        exact_ref[...] = jnp.zeros(exact_ref.shape, exact_ref.dtype)
        lse_ref[...] = jnp.zeros(lse_ref.shape, lse_ref.dtype)

    def arrange(t, unused):
        for half in range(2):
            block = qkv_ref[place_ref[2 * t + half]]
            columns = slice(half * ch, (half + 1) * ch)
            queries[t, :, columns] = block[:HD]
            keys[t, columns, :] = block[HD : 2 * HD].T
            values[t, :, columns] = block[2 * HD :]
        return unused

    lax.fori_loop(0, tiles, arrange, 0)
    scale = log2_e * HD**-0.5

    def query_tile(step, unused):
        t = tiles_ref[step]
        query = queries[t]

        def visit(j, carry, diagonal=False):
            peak, total, acc = carry
            scores = dot(keys[j], query, 1, 0) * scale
            if diagonal:
                scores = jnp.where(down_ref[...] <= along_ref[...], scores, masked_value)
            new_peak = jnp.maximum(peak, jnp.max(scores, axis=0, keepdims=True))
            weights = jnp.exp2(scores - new_peak)
            shrink = jnp.exp2(peak - new_peak)
            total = total * shrink + jnp.sum(weights, axis=0, keepdims=True)
            acc = acc * shrink + dot(values[j], weights.astype(bf16), 1, 0)
            return new_peak, total, acc

        carry = (
            jnp.full((1, span), masked_value, f32),
            jnp.zeros((1, span), f32),
            jnp.zeros((HD, span), f32),
        )
        carry = visit(t, carry, True)
        peak, total, acc = lax.fori_loop(0, t, visit, carry)
        result = acc / total
        lse = peak + jnp.log2(total)
        for half in range(2):
            at = place_ref[2 * t + half]
            columns = slice(half * ch, (half + 1) * ch)
            exact_ref[at] = result[:, columns]
            out_ref[at] = result[:, columns].astype(bf16)
            lse_ref[at] = lse[:, columns]
        return unused

    lax.fori_loop(0, mine, query_tile, 0)


def attend(place, tiles, along, down, qkv):
    blocks, _, ch = qkv.shape
    n = blocks // 2
    return pl.pallas_call(
        attend_kernel,
        in_specs=[smem, smem] + [vmem] * 3,
        out_specs=[vmem] * 3,
        out_shape=[
            jax.ShapeDtypeStruct((blocks, HD, ch), bf16),
            jax.ShapeDtypeStruct((blocks, HD, ch), f32),
            jax.ShapeDtypeStruct((blocks, 1, ch), f32),
        ],
        scratch_shapes=[
            pltpu.VMEM((n, 2 * ch, HD), bf16),
            pltpu.VMEM((n, HD, 2 * ch), bf16),
            pltpu.VMEM((n, HD, 2 * ch), bf16),
        ],
        compiler_params=compiler_params(40),
        cost_estimate=heavy,
    )(place, tiles, along, down, qkv)


def unrotate(values, cosine, sine):
    half = ROT // 2
    first, second = values[:half], values[half:ROT]
    return jnp.concatenate(
        [first * cosine + second * sine, second * cosine - first * sine, values[ROT:]], axis=0
    )


def attend_back_kernel(
    place_ref,
    tiles_ref,
    along_ref,
    down_ref,
    qkv_ref,
    grad_ref,
    exact_ref,
    lse_ref,
    cos_ref,
    sin_ref,
    out_ref,
    sums_ref,
    keys_t,
    keys,
    queries_t,
    queries,
    values,
    grads_t,
    grads,
    lse,
    delta,
    grad_q,
    grad_k,
    grad_v,
):
    blocks, _, ch = qkv_ref.shape
    span = 2 * ch
    tiles = blocks // 2
    mine = tiles_ref.shape[0]

    def arrange(t, unused):
        for half in range(2):
            at = place_ref[2 * t + half]
            block = qkv_ref[at]
            columns = slice(half * ch, (half + 1) * ch)
            queries_t[t, :, columns] = block[:HD]
            queries[t, columns, :] = block[:HD].T
            keys_t[t, :, columns] = block[HD : 2 * HD]
            keys[t, columns, :] = block[HD : 2 * HD].T
            values[t, columns, :] = block[2 * HD :].T
            grad = grad_ref[at]
            grads_t[t, :, columns] = grad
            grads[t, columns, :] = grad.T
            lse[t, :, columns] = lse_ref[at]
            delta[t, :, columns] = jnp.sum(grad.astype(f32) * exact_ref[at], axis=0, keepdims=True)
        grad_q[t] = jnp.zeros(grad_q.shape[1:], f32)
        grad_k[t] = jnp.zeros(grad_k.shape[1:], f32)
        grad_v[t] = jnp.zeros(grad_v.shape[1:], f32)
        return unused

    lax.fori_loop(0, tiles, arrange, 0)
    factor = HD**-0.5
    scale = log2_e * factor

    def query_tile(step, unused):
        t = tiles_ref[step]

        def visit(j, acc, diagonal=False):
            scores = dot(keys[j], queries_t[t], 1, 0) * scale
            weights = jnp.exp2(scores - lse[t])
            if diagonal:
                weights = jnp.where(down_ref[...] <= along_ref[...], weights, 0.0)
            grad_weights = dot(values[j], grads_t[t], 1, 0)
            grad_scores = (weights * (grad_weights - delta[t])).astype(bf16)
            grad_v[j] += dot(weights.astype(bf16), grads[t], 1, 0)
            grad_k[j] += dot(grad_scores, queries[t], 1, 0)
            return acc + dot(keys_t[j], grad_scores, 1, 0)

        acc = visit(t, jnp.zeros((HD, span), f32), True)
        grad_q[t] = lax.fori_loop(0, t, visit, acc)
        return unused

    lax.fori_loop(0, mine, query_tile, 0)

    def finish(t, sums):
        key_t = grad_k[t].T
        value_t = grad_v[t].T
        for half in range(2):
            at = place_ref[2 * t + half]
            columns = slice(half * ch, (half + 1) * ch)
            cosine, sine = cos_ref[2 * t + half], sin_ref[2 * t + half]
            parts = (
                unrotate(grad_q[t][:, columns] * factor, cosine, sine),
                unrotate(key_t[:, columns] * factor, cosine, sine),
                value_t[:, columns],
            )
            rows = jnp.concatenate(parts, axis=0).astype(bf16)
            out_ref[at] = rows
            sums = sums + rows.astype(f32)
        return sums

    sums = lax.fori_loop(0, tiles, finish, jnp.zeros((3 * HD, ch), f32))
    sums_ref[...] = jnp.sum(sums, axis=1, keepdims=True)


def attend_back(place, tiles, along, down, qkv, grad, exact, lse, cosine, sine):
    blocks, _, ch = qkv.shape
    n = blocks // 2
    flat = pltpu.VMEM((n, HD, 2 * ch), bf16)
    tall = pltpu.VMEM((n, 2 * ch, HD), bf16)
    line = pltpu.VMEM((n, 1, 2 * ch), f32)
    return pl.pallas_call(
        attend_back_kernel,
        in_specs=[smem, smem] + [vmem] * 8,
        out_specs=[vmem] * 2,
        out_shape=[
            jax.ShapeDtypeStruct((blocks, 3 * HD, ch), bf16),
            jax.ShapeDtypeStruct((3 * HD, 1), f32),
        ],
        scratch_shapes=[
            flat,
            tall,
            flat,
            tall,
            tall,
            flat,
            tall,
            line,
            line,
            pltpu.VMEM((n, HD, 2 * ch), f32),
            pltpu.VMEM((n, 2 * ch, HD), f32),
            pltpu.VMEM((n, 2 * ch, HD), f32),
        ],
        compiler_params=compiler_params(48),
        cost_estimate=heavy,
    )(place, tiles, along, down, qkv, grad, exact, lse, cosine, sine)


def feed_kernel(order_ref, *refs, pieces):
    rows_in, grads_in = refs[:pieces], refs[pieces]
    gate_hbm, up_hbm, down_hbm = refs[pieces + 1 : pieces + 4]
    hidden_ref, grad_gate_ref, grad_up_ref, rows_ref, grads_ref = refs[pieces + 4 : pieces + 9]
    out_refs, (gate_w, up_w, down_w, sems) = refs[pieces + 9 : -4], refs[-4:]
    pairs = ((gate_hbm, gate_w), (up_hbm, up_w), (down_hbm, down_w))
    copies = [
        pltpu.make_async_copy(source, target, sems.at[k])
        for k, (source, target) in enumerate(pairs)
    ]
    for copy in copies:
        copy.start()
    halves, ch, _ = rows_ref.shape
    count = order_ref.shape[0] - 1
    step = ch // count
    for c in range(halves):
        for k, place in each_piece(rows_in):
            rows_ref[c, place, :] = piece(rows_in, k, c, order_ref[0])
        for k in range(count):
            start = pl.multiple_of(order_ref[1 + k] * step, step)
            grads_ref[c, k * step : (k + 1) * step, :] = grads_in[0, c, pl.ds(start, step), :]
    for c in range(halves):
        if c == 0:
            copies[0].wait()
        gate = dot(rows_ref[c], gate_w[...], 1, 0)
        if c == 0:
            copies[1].wait()
        up_value = dot(rows_ref[c], up_w[...], 1, 0)
        sigmoid_gate = jax.nn.sigmoid(gate)
        silu_gate = gate * sigmoid_gate
        hidden_ref[c] = (silu_gate * up_value).astype(bf16)
        if c == 0:
            copies[2].wait()
        grad_hidden = dot(grads_ref[c], down_w[...], 1, 1)
        grad_up = (grad_hidden * silu_gate).astype(bf16)
        grad_gate = (
            grad_hidden * up_value * sigmoid_gate * (1.0 + gate * (1.0 - sigmoid_gate))
        ).astype(bf16)
        grad_up_ref[c] = grad_up
        grad_gate_ref[c] = grad_gate
        summand = dot(grad_gate, gate_w[...], 1, 1) + dot(grad_up, up_w[...], 1, 1)
        put_pieces(out_refs, c, summand.astype(bf16))


def feed(order, rows, grads, sequence, gate_weight, up_weight, down_weight, cuts):
    _, halves, ch, width = grads.shape
    hidden = gate_weight.shape[1]
    inner = jax.ShapeDtypeStruct((halves, ch, hidden), bf16)
    outer = jax.ShapeDtypeStruct((halves, ch, width), bf16)
    cut = jax.ShapeDtypeStruct((halves, ch // cuts, width), bf16)
    anywhere = pl.BlockSpec(memory_space=pl.ANY)
    weights = (gate_weight, up_weight, down_weight)
    hidden, grad_gate, grad_up, rows, grads, *out = pl.pallas_call(
        functools.partial(feed_kernel, pieces=len(rows)),
        grid=(1,),
        in_specs=[smem]
        + [whole(member.shape) for member in rows]
        + [pl.BlockSpec((1, halves, ch, width), lambda step: (sequence, 0, 0, 0))]
        + [anywhere] * 3,
        out_specs=[whole(inner.shape)] * 3 + [whole(outer.shape)] * 2 + [whole(cut.shape)] * cuts,
        out_shape=[inner] * 3 + [outer] * 2 + [cut] * cuts,
        scratch_shapes=[pltpu.VMEM(weight.shape, bf16) for weight in weights]
        + [pltpu.SemaphoreType.DMA((3,))],
        compiler_params=compiler_params(58),
        cost_estimate=heavy,
    )(order, *rows, grads, *weights)
    return hidden, grad_gate, grad_up, out, rows, grads


def weight_grad_kernel(*refs, pairs):
    total = dot(refs[0][...], refs[1][...], 0, 0)
    for k in range(1, pairs):
        total = total + dot(refs[2 * k][...], refs[2 * k + 1][...], 0, 0)
    refs[-1][...] = total.astype(bf16)


def weight_grad(lefts, rights, cost=light):
    lefts = [member.reshape(-1, member.shape[-1]) for member in lefts]
    rights = [member.reshape(-1, member.shape[-1]) for member in rights]
    rows, height = lefts[0].shape
    width = rights[0].shape[1]
    if height > width:
        block = min(512, height)
        steps = height // block
        specs = [
            pl.BlockSpec((rows, block), lambda step: (0, step)),
            pl.BlockSpec((rows, width), lambda step: (0, 0)),
        ]
        out = pl.BlockSpec((block, width), lambda step: (step, 0))
    else:
        block = min(512, width)
        steps = width // block
        specs = [
            pl.BlockSpec((rows, height), lambda step: (0, 0)),
            pl.BlockSpec((rows, block), lambda step: (0, step)),
        ]
        out = pl.BlockSpec((height, block), lambda step: (0, step))
    return pl.pallas_call(
        functools.partial(weight_grad_kernel, pairs=len(lefts)),
        grid=(steps,),
        in_specs=specs * len(lefts),
        out_specs=out,
        out_shape=jax.ShapeDtypeStruct((height, width), bf16),
        compiler_params=compiler_params(48),
        cost_estimate=cost,
    )(*[member for pair in zip(lefts, rights) for member in pair])


def split_grad_kernel(at_ref, *refs, pairs, by_rows, added):
    total = dot(refs[0][...], refs[1][...], 0, 0)
    for k in range(1, pairs):
        total = total + dot(refs[2 * k][...], refs[2 * k + 1][...], 0, 0)
    keep_ref, send_ref = refs[-2:]
    size = keep_ref.shape[1 if by_rows else 2]
    if by_rows:
        first, second = total[:size], total[size:]
    else:
        first, second = total[:, :size], total[:, size:]
    low = at_ref[1] == 0
    keep, send = jnp.where(low, first, second), jnp.where(low, second, first)
    if added:
        keep = keep + refs[2 * pairs][0].astype(f32)
        send = send + refs[2 * pairs + 1][0].astype(f32)
    keep_ref[0] = keep.astype(bf16)
    send_ref[0] = send.astype(bf16)


def split_grad(at, lefts, rights, planes, earlier=()):
    lefts = [member.reshape(-1, member.shape[-1]) for member in lefts]
    rights = [member.reshape(-1, member.shape[-1]) for member in rights]
    rows, height = lefts[0].shape
    width = rights[0].shape[1]
    by_rows = height > width
    if by_rows:
        block = height // planes
        specs = [
            pl.BlockSpec((rows, block), lambda step, at: (0, step)),
            pl.BlockSpec((rows, width), lambda step, at: (0, 0)),
        ]
        part = (block // 2, width)
    else:
        block = width // planes
        specs = [
            pl.BlockSpec((rows, height), lambda step, at: (0, 0)),
            pl.BlockSpec((rows, block), lambda step, at: (0, step)),
        ]
        part = (height, block // 2)
    out = pl.BlockSpec((1,) + part, lambda step, at: (step ^ at[0], 0, 0))
    shape = jax.ShapeDtypeStruct((planes,) + part, bf16)
    return pl.pallas_call(
        functools.partial(
            split_grad_kernel, pairs=len(lefts), by_rows=by_rows, added=len(earlier) > 0
        ),
        grid_spec=pltpu.PrefetchScalarGridSpec(
            num_scalar_prefetch=1,
            grid=(planes,),
            in_specs=specs * len(lefts) + [out] * len(earlier),
            out_specs=[out, out],
        ),
        out_shape=[shape, shape],
        compiler_params=compiler_params(48),
        cost_estimate=light,
    )(at, *[member for pair in zip(lefts, rights) for member in pair], *earlier)


def split_first(keep, send):
    other = paired(send, "core", 1)
    return [
        (keep[k].astype(f32) + other[k].astype(f32)).astype(bf16) for k in range(keep.shape[0])
    ]


def split_rest(sums):
    return sums[:1] + [paired(sums[step], "plane", step) for step in range(1, len(sums))]


def split_whole(sums):
    total = sums[0].astype(f32)
    for member in sums[1:]:
        total = total + member.astype(f32)
    return total


def feed_out_kernel(order_ref, *refs):
    hidden, weight_ref, out_ref = refs[:-2], refs[-2], refs[-1]
    halves, ch, _ = hidden[0].shape
    count = order_ref.shape[0] - 1
    step = ch // count
    for s, ref in enumerate(hidden):
        for c in range(halves):
            result = dot(ref[c], weight_ref[...], 1, 0).astype(bf16)
            for k in range(count):
                start = pl.multiple_of(order_ref[1 + k] * step, step)
                out_ref[s * halves + c, pl.ds(start, step), :] = result[k * step : (k + 1) * step]


def feed_out(order, hidden, weight):
    halves, ch, _ = hidden[0].shape
    inner, width = weight.shape
    block = min(512, width)
    count = len(hidden) * halves
    return pl.pallas_call(
        feed_out_kernel,
        grid=(width // block,),
        in_specs=[smem]
        + [whole(member.shape) for member in hidden]
        + [pl.BlockSpec((inner, block), lambda step: (0, step))],
        out_specs=pl.BlockSpec((count, ch, block), lambda step: (0, 0, step)),
        out_shape=jax.ShapeDtypeStruct((count, ch, width), bf16),
        compiler_params=compiler_params(40),
        cost_estimate=light,
    )(order, *hidden, weight)


def local(
    layer_input,
    block_order,
    first_gain,
    first_shift,
    query_weight,
    key_weight,
    value_weight,
    query_bias,
    key_bias,
    value_bias,
    out_weight,
    second_gain,
    second_shift,
    gate_weight,
    up_weight,
    down_weight,
    out_grad,
):
    seqs, _, halves, part_rows, width = layer_input.shape
    planes = lax.axis_size("plane")
    devices = 2 * planes
    head_size = lax.axis_size("head")
    blk = lax.axis_index("plane") * 2 + lax.axis_index("core")
    head_index = lax.axis_index("head")
    blk_scalar = blk.astype(jnp.int32).reshape(1)
    ends = ends_chain().reshape(1)
    cuts = head_size if in_chain() else 1
    where = jnp.concatenate([blk_scalar, ends])
    order = jnp.concatenate([ends, head_order()])
    ch = part_rows * head_size
    blocks = halves * devices
    heads = query_bias.shape[0]
    local_width = heads * HD
    copies = devices // heads

    part = first_gain.shape[0]
    q_dims, k_dims = query_bias.shape[1], key_bias.shape[1]
    small = jnp.concatenate(
        [first_gain, first_shift, second_gain, second_shift]
        + [member.reshape(-1) for member in (query_bias, key_bias, value_bias)]
    )

    owner = jnp.arange(devices, dtype=jnp.int32) ^ blk
    first_id = block_order[owner]
    rank = jnp.stack([first_id, 2 * devices - 1 - first_id], axis=1).reshape(-1)
    place = jnp.zeros((blocks,), jnp.int32).at[rank].set(jnp.arange(blocks, dtype=jnp.int32))
    offsets = head_offsets(part_rows)
    own_positions = rank[:halves, None] * ch + offsets[None, :]
    cos_own, sin_own = rotary_tables(own_positions)
    all_positions = jnp.arange(blocks, dtype=jnp.int32)[:, None] * ch + offsets[None, :]
    cos_all, sin_all = rotary_tables(all_positions)
    along = all_positions[:2].reshape(1, -1)
    down = all_positions[:2].reshape(-1, 1)
    tile_count = blocks // 2
    cycle = jnp.arange(tile_count // copies, dtype=jnp.int32)
    share = blk % copies
    tiles = (cycle // 2) * 2 * copies + jnp.where(cycle % 2 == 0, share, 2 * copies - 1 - share)
    if copies == 1:
        tiles = jnp.arange(tile_count, dtype=jnp.int32)

    core = lax.axis_index("core").astype(jnp.int32)
    at = jnp.stack([lax.axis_index("plane").astype(jnp.int32), core])

    full_qkv = blk_gather(jnp.concatenate([query_weight, key_weight, value_weight], axis=1))
    full_out = blk_gather(out_weight, 1)

    def split_small(small):
        small = small_gather(in_head_order(gather_whole(small)[0], 0), BLK).astype(f32)
        gain_one, shift_one, gain_two, shift_two = [
            small[:, k * part : (k + 1) * part].reshape(1, -1) for k in range(4)
        ]
        biases = lax.dynamic_index_in_dim(
            small[:, 4 * part :].reshape(devices, head_size, -1), head_index, 1, keepdims=False
        )

        def bias_of(start, dims):
            member = biases[:, start : start + heads * dims].reshape(devices, heads, dims)
            return jnp.swapaxes(member, 0, 1).reshape(heads, devices * dims)

        bias_query = bias_of(0, q_dims)
        bias_key = jnp.pad(bias_of(heads * q_dims, k_dims), ((0, 0), (0, HD - ROT)))
        bias_value = bias_of(heads * (q_dims + k_dims), q_dims)
        bias = jnp.concatenate([bias_query, bias_key, bias_value], axis=0).reshape(1, -1)
        return gain_one, shift_one, gain_two, shift_two, bias

    each = range(seqs)
    inputs = [layer_input[s, 0] for s in each]
    grad_own = [out_grad[s, 0] for s in each]

    def queries_of(pieces):
        return project_in(
            where, pieces, gain_one, shift_one, full_qkv, bias, cos_own, sin_own, devices
        )

    def move_first(value, rows):
        return exchange_first(value.reshape(devices, halves, rows, ch))

    def move(value, rows):
        return exchange_rest(move_first(value, rows))

    def flat(member):
        return member.reshape(-1, member.shape[-1])

    def attend_of(qkv):
        return attend(place, tiles, along, down, qkv.reshape(blocks, 3 * HD, ch))

    def attend_back_of(qkv, attended, grad):
        _, exact, lse = attended
        grad = grad.reshape(blocks, HD, ch)
        qkv = qkv.reshape(blocks, 3 * HD, ch)
        return attend_back(place, tiles, along, down, qkv, grad, exact, lse, cos_all, sin_all)

    stage = lax.optimization_barrier
    in_a, in_b = inputs
    grad_own_a, grad_own_b = grad_own
    small = gather_direct(small[None, None])
    got = gather_first(in_a)
    in_a, got, in_b, small = stage((in_a, got, in_b, small))
    parts = gather_rest(in_a, got)
    parts, in_b, cos_own, sin_own, (gain_one, shift_one, gain_two, shift_two, bias) = stage(
        (parts, in_b, cos_own, sin_own, split_small(small))
    )
    x_a = gather_pieces(parts)
    got = gather_first(in_b)
    qkv_a, one_a = queries_of(x_a)
    got, in_b, x_a, one_a, qkv_a = stage((got, in_b, x_a, one_a, qkv_a))
    parts = gather_rest(in_b, got)
    qkv_a = move(qkv_a, 3 * HD)
    parts, own_grads = stage((parts, out_grad))
    grads = lax.all_gather(own_grads[:, 0], "head", axis=2, tiled=True)
    x_b = gather_pieces(parts)
    made, one_b = queries_of(x_b)
    qkv_a, x_b, one_b, made, late = stage(
        (qkv_a, x_b, one_b, made, (gate_weight, up_weight, down_weight))
    )
    full_gate, full_up, full_down = blk_gather(late[0]), blk_gather(late[1]), blk_gather(late[2], 1)
    made = move_first(made, 3 * HD)
    made, qkv_a = stage((made, qkv_a))
    qkv_b = exchange_rest(made)
    att_a = attend_of(qkv_a)
    qkv_b, att_a = stage((qkv_b, att_a))
    att = move(att_a[0], HD)
    att, qkv_b = stage((att, qkv_b))
    partial, out_a = project_out(blk_scalar, att, full_out, cuts)
    sums = scatter_first(partial)
    att_b = attend_of(qkv_b)
    sums, att_b, out_a = stage((sums, att_b, out_a))
    sums = scatter_rest(sums)
    att = move(att_b[0], HD)
    partial, out_b = project_out(blk_scalar, att, full_out, cuts)
    sums, partial, out_b = stage((sums, partial, out_b))
    middle_a, normed = middle_of(scatter_pieces(sums), in_a, gain_two, shift_two)
    got = gather_first(normed)
    sums = scatter_first(partial)
    got, sums, normed, middle_a = stage((got, sums, normed, middle_a))
    parts = gather_rest(normed, got)
    sums = scatter_rest(sums)
    parts, sums = stage((parts, sums))
    middle_b, normed = middle_of(scatter_pieces(sums), in_b, gain_two, shift_two)
    got = gather_first(normed)
    feeding = feed(
        order, gather_pieces(parts), grads, 0, full_gate, full_up, full_down, cuts
    )
    got, normed, middle_b, feeding = stage((got, normed, middle_b, feeding))
    hid_a, gate_a, up_a, partial, two_a, og_a = feeding
    sums = scatter_first(partial)
    parts = gather_rest(normed, got)
    parts, sums = stage((parts, sums))
    sums = scatter_rest(sums)
    feeding = feed(
        order, gather_pieces(parts), grads, 1, full_gate, full_up, full_down, cuts
    )
    sums, feeding, hid_a = stage((sums, feeding, hid_a))
    hid_b, gate_b, up_b, partial, two_b, og_b = feeding
    mid_grad_a, branch_a, gain_two_a, shift_two_a = back_two(
        scatter_pieces(sums), middle_a, grad_own_a, gain_two
    )
    got = gather_first(branch_a)
    sums = scatter_first(partial)
    down_grad = weight_grad((hid_a, hid_b), (og_a, og_b))
    got, sums, down_grad, branch_a, mid_grad_a, gate_a, up_a, hid_a = stage(
        (got, sums, down_grad, branch_a, mid_grad_a, gate_a, up_a, hid_a)
    )
    down_grad = blk_scatter(down_grad, 1)
    parts = gather_rest(branch_a, got)
    sums = scatter_rest(sums)
    gate_grad = weight_grad((two_a, two_b), (gate_a, gate_b))
    gate_grad, up_a = stage((gate_grad, up_a))
    up_grad = weight_grad((two_a, two_b), (up_a, up_b))
    up_grad, hid_a = stage((up_grad, hid_a))
    feeds = feed_out(order, (hid_a, hid_b), full_down)
    parts, sums, gate_grad, feeds, up_grad = stage((parts, sums, gate_grad, feeds, up_grad))
    gate_grad = blk_scatter(gate_grad)
    mid_grad_b, branch_b, gain_two_b, shift_two_b = back_two(
        scatter_pieces(sums), middle_b, grad_own_b, gain_two
    )
    branch_b, parts, mid_grad_b = stage((branch_b, parts, mid_grad_b))
    got = gather_direct(branch_b)
    att_grad_a, whole_a = project_grad(where, gather_pieces(parts), full_out, devices, ch)
    att_grad_a = move(att_grad_a, HD)
    branch_b, mid_grad_b, whole_a, att_grad_a, feeds, up_grad = stage(
        (branch_b, mid_grad_b, whole_a, att_grad_a, feeds, up_grad)
    )
    feeds = lax.psum_scatter(feeds, "head", scatter_dimension=1, tiled=True)
    made_a, bias_sums_a = attend_back_of(qkv_a, att_a, att_grad_a)
    got, made_a, whole_a, up_grad = stage((got, made_a, whole_a, up_grad))
    att_grad_b, whole_b = project_grad(where, gather_pieces(got), full_out, devices, ch)
    att_grad_b = move_first(att_grad_b, HD)
    moved = move_first(made_a, 3 * HD)
    att_grad_b, moved, whole_b = stage((att_grad_b, moved, whole_b))
    att_grad_b = exchange_rest(att_grad_b)
    out_weight_grad = weight_grad((out_a, out_b), (whole_a, whole_b))
    moved, att_grad_b, up_grad, out_weight_grad = stage(
        (moved, att_grad_b, up_grad, out_weight_grad)
    )
    moved = exchange_rest(moved)
    made_b, bias_sums_b = attend_back_of(qkv_b, att_b, att_grad_b)
    moved, made_b, out_weight_grad, up_grad = stage((moved, made_b, out_weight_grad, up_grad))
    up_grad = blk_scatter(up_grad)
    out_weight_grad = blk_scatter(out_weight_grad, 1)
    moved_b = move_first(made_b, 3 * HD)
    moved, moved_b, down_grad, gate_grad = stage((moved, moved_b, down_grad, gate_grad))
    down_grad, gate_grad = down_grad.astype(f32), gate_grad.astype(f32)
    moved_b = exchange_rest(moved_b)
    partial, qkv_rows_a, gain_one_a, shift_one_a = project_back(where, x_a, moved, full_qkv, cuts)
    sums_a = scatter_first(partial)
    moved_b, sums_a, down_grad, gate_grad, feeds = stage(
        (moved_b, sums_a, down_grad, gate_grad, feeds)
    )
    partial, qkv_rows_b, gain_one_b, shift_one_b = project_back(where, x_b, moved_b, full_qkv, cuts)
    partial, qkv_rows_b, sums_a = stage((partial, qkv_rows_b, sums_a))
    sums_a = scatter_rest(sums_a)
    sums_b = scatter_first(partial)
    qkv_split = split_grad(at, (one_a, one_b), (qkv_rows_a, qkv_rows_b), planes)
    sums_a, sums_b, qkv_split = stage((sums_a, sums_b, qkv_split))
    sums_b = scatter_rest(sums_b)

    norm_one_grads = ((gain_one_a, shift_one_a), (gain_one_b, shift_one_b))
    norm_two_grads = ((gain_two_a, shift_two_a), (gain_two_b, shift_two_b))
    bias_sums = (bias_sums_a, bias_sums_b)

    def over_all(grads, k):
        total = grads[0][k]
        for s in range(1, seqs):
            total = total + grads[s][k]
        return total.reshape(devices * head_size, part)

    bias_total = bias_sums[0]
    for s in range(1, seqs):
        bias_total = bias_total + bias_sums[s]
    bias_total = bias_total.reshape(3, HD)
    shares = jnp.concatenate(
        [
            bias_total[0].reshape(devices, q_dims),
            bias_total[1, :ROT].reshape(devices, k_dims),
            bias_total[2].reshape(devices, q_dims),
        ],
        axis=1,
    )
    own_head = (jnp.arange(heads, dtype=jnp.int32) == blk // copies).astype(f32)
    own_column = (jnp.arange(head_size, dtype=jnp.int32) == head_index).astype(f32)
    spread = (
        shares[:, None, None, :] * own_head[None, None, :, None] * own_column[None, :, None, None]
    ).reshape(devices * head_size, -1)
    smalls = jnp.concatenate(
        [
            over_all(norm_one_grads, 0),
            over_all(norm_one_grads, 1),
            over_all(norm_two_grads, 0),
            over_all(norm_two_grads, 1),
            spread,
        ],
        axis=1,
    )
    smalls = small_scatter(smalls.reshape(devices, head_size, -1), BLK)
    qkv_split = split_first(*qkv_split)
    qkv_split = split_rest(qkv_split)
    input_grad_a = back_one(scatter_pieces(sums_a), in_a, mid_grad_a, gain_one)
    feeds = feeds.astype(f32)
    layer_output = jnp.stack([middle_a + feeds[:halves], middle_b + feeds[halves:]])[:, None]
    sums_b, smalls, input_grad_a, qkv_split, layer_output, out_weight_grad = stage(
        (sums_b, smalls, input_grad_a, qkv_split, layer_output, out_weight_grad)
    )
    up_grad = up_grad.astype(f32)
    smalls = small_scatter(smalls, ALL[2:])
    qkv_grad = split_whole(qkv_split)
    out_weight_grad = out_weight_grad.astype(f32)

    norm_grads = [smalls[k * part : (k + 1) * part] for k in range(4)]
    bias_grads = smalls[4 * part :].reshape(heads, 2 * q_dims + k_dims)
    input_grad_b = back_one(scatter_pieces(sums_b), in_b, mid_grad_b, gain_one)
    input_grad = jnp.stack([input_grad_a, input_grad_b])[:, None]
    return (
        layer_output,
        input_grad,
        norm_grads[0],
        norm_grads[1],
        qkv_grad[:, :local_width],
        qkv_grad[:, local_width : 2 * local_width],
        qkv_grad[:, 2 * local_width :],
        bias_grads[:, :q_dims],
        bias_grads[:, q_dims : q_dims + k_dims],
        bias_grads[:, q_dims + k_dims :],
        out_weight_grad,
        norm_grads[2],
        norm_grads[3],
        gate_grad,
        up_grad,
        down_grad,
    )


def solution(mesh):
    blk_size, head_size = mesh.devices.shape
    split = Mesh(mesh.devices.reshape(blk_size // 2, 2, head_size), ALL)
    tokens = P(None, BLK, None, "head", None)
    rows = P(BLK, "head")
    columns = P("head", BLK)
    return jax.shard_map(
        local,
        mesh=split,
        in_specs=(
            tokens,
            P(),
            P(ALL),
            P(ALL),
            rows,
            rows,
            rows,
            columns,
            columns,
            columns,
            columns,
            P(ALL),
            P(ALL),
            rows,
            rows,
            columns,
            tokens,
        ),
        out_specs=(
            tokens,
            tokens,
            P(ALL),
            P(ALL),
            rows,
            rows,
            rows,
            columns,
            columns,
            columns,
            columns,
            P(ALL),
            P(ALL),
            rows,
            rows,
            columns,
        ),
        check_vma=False,
    )
```
